128 devices in a mesh: role: 2 (over core), row: 4 (over x), col: 16 (over z, y).
Axes of the slice: x: 4, y: 4, z: 4, core: 2. Of those that a mesh axis runs over, the one named last changes fastest.
Arguments:
- queries: bfloat16 [128, 32, 4096], P(('role', 'row', 'col')), may hold values from -6 to 6
- cache_keys: bfloat16 [128, 4096, 512], P(('role', 'row', 'col')), may hold values from -6 to 6
- prompt_value_cache: bfloat16 [128, 4096, 512], P(('role', 'row', 'col')), may hold values from -6 to 6
- new_keys: bfloat16 [128, 32, 512], P(('role', 'row', 'col')), may hold values from -6 to 6
- fresh_token_values: bfloat16 [128, 32, 512], P(('role', 'row', 'col')), may hold values from -6 to 6
- hidden: bfloat16 [128, 32, 2048], P(('role', 'row', 'col')), may hold values from -6 to 6
- out_weight: bfloat16 [4096, 2048], P('row'), may hold values from -0.09375 to 0.09375
- norm_gain: float32 [2048], replicated, may hold values from 0.1 to 1.9
- expert_gate: bfloat16 [128, 2048, 768], P(('role', 'row', 'col')), may hold values from -0.125 to 0.125
- expert_up: bfloat16 [128, 2048, 768], P(('role', 'row', 'col')), may hold values from -0.125 to 0.125
- expert_down: bfloat16 [128, 768, 2048], P(('role', 'row', 'col')), may hold values from -0.21875 to 0.21875
- expert_ids: int32 [128, 32, 8], P(('role', 'row', 'col')), may hold values from 0 to 127, all different within a row; in each aligned block of 32 rows (0 to 31, 32 to 63, ..., all dimensions but the last counted through in order) at most 5 rows name the same one
- routing_gates: float32 [128, 32, 8], P(('role', 'row', 'col')), may hold values from 0.1 to 1
Outputs:
- layer_out: bfloat16 [128, 32, 2048], P(('role', 'row', 'col'))
The draws below stay inside these ranges and needn't reach their ends.
Inputs may be any that keep to these rules, and one draw needn't show every extreme that they name: `expert_ids`: each row names 8 different experts; in the 32 rows of one prompt no expert is named more than 5 times, a bound that some block reaches; every expert is named by some row.
All inputs are finite; a program needn't handle non-finite values.
Results may differ from the reference program's by a relative error of at most 0.014.
Values may be sent and summed in bfloat16 or wider, within the bound.
A program may use at most 128 MiB of HBM per device.

```python
import math
import jax
import jax.numpy as jnp
import numpy as np
from jax import lax

D = 2048
QUERY_HEADS = 32
KEY_VALUE_HEADS = 4
HEAD_SIZE = 128
FE = 768
TOP = 8
RESPONSE_COUNT = 32
CACHED_TOKENS = 4096
PROMPT_COUNT = 128
EXPERTS = 128
CAP = 5


def starting_queries(key):
    gaussian_component = jax.random.normal(jax.random.fold_in(key, 101), (PROMPT_COUNT, RESPONSE_COUNT, QUERY_HEADS * HEAD_SIZE), jnp.float32)
    return jnp.clip(1.5 * gaussian_component, -6.0, 6.0)


def draw_queries(key, part):
    value_rows = starting_queries(key)
    return value_rows.astype(jnp.bfloat16)


def draw_cache_keys(key, part):
    gaussian_component = jax.random.normal(jax.random.fold_in(key, 103), (PROMPT_COUNT, CACHED_TOKENS, KEY_VALUE_HEADS * HEAD_SIZE), jnp.float32)
    value_rows = jnp.clip(gaussian_component, -6.0, 6.0)
    return value_rows.astype(jnp.bfloat16)


def draw_new_keys(key, part):
    query_foundation = starting_queries(key).reshape(PROMPT_COUNT, RESPONSE_COUNT, KEY_VALUE_HEADS, QUERY_HEADS // KEY_VALUE_HEADS, HEAD_SIZE)
    gaussian_component = jax.random.normal(jax.random.fold_in(key, 104), (PROMPT_COUNT, RESPONSE_COUNT, KEY_VALUE_HEADS, HEAD_SIZE), jnp.float32)
    value_rows = 2.3 * jnp.mean(query_foundation, axis=3) + 0.5 * gaussian_component
    value_rows = jnp.clip(value_rows, -6.0, 6.0)
    return value_rows.reshape(PROMPT_COUNT, RESPONSE_COUNT, KEY_VALUE_HEADS * HEAD_SIZE).astype(jnp.bfloat16)


def block_scale(key, extent, cuts, least, top_value):
    factor_of, own = 1.0, jax.random.fold_in(key, 6)
    for dim, shards_of in cuts:
        steps = jnp.exp(jax.random.uniform(jax.random.fold_in(own, dim), (shards_of,), jnp.float32, least / len(cuts), top_value / len(cuts)))
        factor_of = factor_of * jnp.repeat(steps, extent[dim] // shards_of).reshape([-1 if axis == dim else 1 for axis in range(len(extent))])
    return factor_of


def shared_out(stream_key, own, number, rows, number_of, top, reach, lean):
    ranking = jax.random.permutation(stream_key, number_of)
    packed, common = shares(number_of, rows * top, reach, lean, True), shares(number_of, rows * top, reach, lean, False)
    places = jnp.arange(number_of)

    def named(tallies, rotation):
        used = int((tallies > 0).sum())
        fixed = max(1, used // 4)
        moved = fixed + (places - fixed + rotation * (used - fixed)) % max(1, number_of - fixed)
        return jnp.zeros((number_of,), jnp.int32).at[ranking[jnp.where(places < fixed, places, moved)]].set(jnp.asarray(tallies, jnp.int32))

    tallies = jnp.where(number % 4 == 0, named(packed, number // 4), named(common, number - number // 4 - 1))
    mixed = jax.random.permutation(jax.random.fold_in(own, 3), number_of)
    donor, taker = mixed[0:number_of // 2 * 2:2], mixed[1:number_of // 2 * 2:2]
    slack = jnp.minimum(tallies[donor] - 1, reach - tallies[taker]) // 2
    slack = jnp.where((donor == ranking[0]) | (taker == ranking[0]) | (tallies[taker] == 0), 0, jnp.maximum(slack, 0))
    moved = jax.random.randint(jax.random.fold_in(own, 4), (number_of // 2,), 0, 1 << 20) % (slack + 1)
    tallies = tallies.at[donor].add(-moved).at[taker].add(moved)
    items = jnp.searchsorted(jnp.cumsum(tallies), jnp.arange(rows * top), side="right").astype(jnp.int32)
    table = items.reshape(top, rows).T
    table = table[jax.random.permutation(jax.random.fold_in(own, 1), rows)]
    rotation = jax.random.randint(jax.random.fold_in(own, 2), (rows, 1), 0, top)
    return jnp.take_along_axis(table, (jnp.arange(top)[None, :] + rotation) % top, axis=1)


def shares(amount, total, most, lean, full):
    loads = [(1 << 20) // math.isqrt(grade ** lean) + 1 for grade in range(1, amount + 1)]
    largest = most if full else min(most, max(-(-total // amount), total * loads[0] // sum(loads)))
    least = 1 if total - largest >= amount - 1 else 0
    given, surplus = [largest] + [least] * (amount - 1), total - largest - least * (amount - 1)
    while surplus > 0:
        free = [i for i in range(1, amount) if given[i] < largest] or [i for i in range(1, amount) if given[i] < most]
        whole, left = sum([loads[i] for i in free]), surplus
        for i in free:
            more = min(most - given[i], max(1, left * loads[i] // whole), surplus)
            given[i] = given[i] + more
            surplus = surplus - more
    return np.array(given)


def centred(key, dims, deviation, bound, cuts=(), kind=jnp.bfloat16):
    drawn = jax.random.normal(key, dims, jnp.float32) * deviation
    if len(cuts) > 0:
        drawn = block_scale(key, dims, cuts, -0.22, 0.18) * drawn
    return jnp.clip(drawn, min=-bound, max=bound).astype(kind)


def setup_inputs(seed: int = 0) -> dict:
    arg_keys = jax.random.split(jax.random.key(seed), 14)
    queries = draw_queries(jax.random.fold_in(arg_keys[13], 71), 0)
    cache_keys = draw_cache_keys(jax.random.fold_in(arg_keys[13], 71), 0)
    prompt_value_cache = centred(arg_keys[2], (PROMPT_COUNT, CACHED_TOKENS, KEY_VALUE_HEADS * HEAD_SIZE), 1.0, 6.0, ((0, 128),))
    new_keys = draw_new_keys(jax.random.fold_in(arg_keys[13], 71), 0)
    fresh_token_values = centred(arg_keys[4], (PROMPT_COUNT, RESPONSE_COUNT, KEY_VALUE_HEADS * HEAD_SIZE), 1.0, 6.0, ((0, 128),))
    hidden = centred(arg_keys[5], (PROMPT_COUNT, RESPONSE_COUNT, D), 1.0, 6.0, ((0, 128),))
    out_weight = centred(arg_keys[6], (QUERY_HEADS * HEAD_SIZE, D), (QUERY_HEADS * HEAD_SIZE) ** -0.5, 0.09375, ((0, 4),))
    norm_gain = jnp.clip(1.0 + 0.18 * jax.random.normal(arg_keys[7], (D,), jnp.float32), 0.1, 1.9)
    expert_gate = centred(arg_keys[8], (EXPERTS, D, FE), D ** -0.5, 0.125, ((0, 128),))
    expert_up = centred(arg_keys[9], (EXPERTS, D, FE), D ** -0.5, 0.125, ((0, 128),))
    expert_down = centred(arg_keys[10], (EXPERTS, FE, D), FE ** -0.5, 0.21875, ((0, 128),))
    expert_ids_keys = jax.random.split(jax.random.fold_in(arg_keys[11], 1), PROMPT_COUNT * RESPONSE_COUNT // RESPONSE_COUNT)
    expert_ids_turns = jax.random.permutation(jax.random.fold_in(arg_keys[11], 3), PROMPT_COUNT * RESPONSE_COUNT // RESPONSE_COUNT)
    expert_ids = jax.vmap(lambda own, number: shared_out(jax.random.fold_in(arg_keys[11], 2), own, number, RESPONSE_COUNT, EXPERTS, TOP, CAP, 2))(expert_ids_keys, expert_ids_turns).reshape((PROMPT_COUNT, RESPONSE_COUNT, TOP))
    routing_gates = jnp.clip(jnp.exp(math.log(1.0) - 2.3025851 * jax.random.uniform(arg_keys[12], (PROMPT_COUNT, RESPONSE_COUNT, TOP), jnp.float32) ** block_scale(arg_keys[12], (PROMPT_COUNT, RESPONSE_COUNT, TOP), ((0, 128),), -0.2, 0.2)), 0.1, 1.0)
    return dict(queries=queries, cache_keys=cache_keys, prompt_value_cache=prompt_value_cache, new_keys=new_keys, fresh_token_values=fresh_token_values, hidden=hidden, out_weight=out_weight, norm_gain=norm_gain, expert_gate=expert_gate, expert_up=expert_up, expert_down=expert_down, expert_ids=expert_ids, routing_gates=routing_gates)


def attend_prompt(operands):
    query_rows, keys_cache, values_cache, keys_new, values_new = operands
    heads_per_group = QUERY_HEADS // KEY_VALUE_HEADS
    score_scale = HEAD_SIZE ** (-0.5)
    pieces = []
    for key_value_head in range(KEY_VALUE_HEADS):
        first_col = key_value_head * heads_per_group * HEAD_SIZE
        q_block = query_rows[:, first_col:first_col + heads_per_group * HEAD_SIZE].reshape(RESPONSE_COUNT * heads_per_group, HEAD_SIZE)
        k_block = keys_cache[:, key_value_head * HEAD_SIZE:(key_value_head + 1) * HEAD_SIZE]
        v_block = values_cache[:, key_value_head * HEAD_SIZE:(key_value_head + 1) * HEAD_SIZE]
        own_key = jnp.repeat(keys_new[:, key_value_head * HEAD_SIZE:(key_value_head + 1) * HEAD_SIZE], heads_per_group, axis=0)
        own_value = jnp.repeat(values_new[:, key_value_head * HEAD_SIZE:(key_value_head + 1) * HEAD_SIZE], heads_per_group, axis=0)
        scores = jnp.dot(q_block, k_block.T, preferred_element_type=jnp.float32) * score_scale
        own_score = lax.optimization_barrier(jnp.sum(q_block.astype(jnp.float32) * own_key.astype(jnp.float32), axis=1)) * score_scale
        highest = jnp.maximum(lax.optimization_barrier(jnp.max(scores, axis=1)), own_score)
        exp_scores = jnp.exp(scores - highest[:, None])
        own_exp = jnp.exp(own_score - highest)
        denominator = lax.optimization_barrier(jnp.sum(exp_scores, axis=1)) + own_exp
        weights = (exp_scores / denominator[:, None]).astype(jnp.bfloat16)
        own_weight = (own_exp / denominator).astype(jnp.bfloat16)
        mixed_rows = jnp.dot(weights, v_block, preferred_element_type=jnp.float32)
        mixed_rows = mixed_rows + own_weight.astype(jnp.float32)[:, None] * own_value.astype(jnp.float32)
        pieces.append(mixed_rows.astype(jnp.bfloat16).reshape(RESPONSE_COUNT, heads_per_group * HEAD_SIZE))
    return jnp.concatenate(pieces, axis=1)

def reference(queries, cache_keys, prompt_value_cache, new_keys, fresh_token_values, hidden, out_weight, norm_gain, expert_gate, expert_up, expert_down, expert_ids, routing_gates):
    attended = lax.map(attend_prompt, (queries, cache_keys, prompt_value_cache, new_keys, fresh_token_values))
    projected = jnp.dot(attended.reshape(PROMPT_COUNT * RESPONSE_COUNT, QUERY_HEADS * HEAD_SIZE), out_weight, preferred_element_type=jnp.float32)
    mid_rows = hidden.reshape(PROMPT_COUNT * RESPONSE_COUNT, D).astype(jnp.float32) + projected
    mean_square = lax.optimization_barrier(jnp.mean(mid_rows * mid_rows, axis=1, keepdims=True))
    normed = (mid_rows * lax.rsqrt(mean_square + 1e-06) * norm_gain[None, :]).astype(jnp.bfloat16)
    normed_three = normed.reshape(PROMPT_COUNT, RESPONSE_COUNT, D)
    flat_ids = expert_ids.reshape(PROMPT_COUNT, RESPONSE_COUNT * TOP).astype(jnp.int32)
    onehot = (flat_ids[:, :, None] == jnp.arange(EXPERTS, dtype=jnp.int32)[None, None, :]).astype(jnp.int32)
    rank_before = jnp.cumsum(onehot, axis=1) - onehot
    slot_index = lax.optimization_barrier(jnp.sum(rank_before * onehot, axis=2)).astype(jnp.int32)
    position = (flat_ids * CAP + slot_index).astype(jnp.int32)
    pair_rows = jnp.broadcast_to((jnp.arange(RESPONSE_COUNT * TOP, dtype=jnp.int32) // TOP)[None, :], (PROMPT_COUNT, RESPONSE_COUNT * TOP))
    prompt_ids = jnp.broadcast_to(jnp.arange(PROMPT_COUNT, dtype=jnp.int32)[:, None], (PROMPT_COUNT, RESPONSE_COUNT * TOP))
    sources = jnp.full((PROMPT_COUNT, EXPERTS * CAP), -1, jnp.int32).at[prompt_ids, position].set(pair_rows)

    def serve_expert(operands):
        expert_num, gate_matrix, up_matrix, down_matrix = operands
        table_rows = lax.dynamic_slice_in_dim(sources, (expert_num * CAP).astype(jnp.int32), CAP, 1)
        safe_rows = jnp.maximum(table_rows, 0).astype(jnp.int32)
        block = jnp.take_along_axis(normed_three, safe_rows[:, :, None], axis=1)
        block = jnp.where((table_rows >= 0)[:, :, None], block, jnp.zeros_like(block))
        flat_block = block.reshape(PROMPT_COUNT * CAP, D)
        gate_part = jnp.dot(flat_block, gate_matrix, preferred_element_type=jnp.float32)
        up_part = jnp.dot(flat_block, up_matrix, preferred_element_type=jnp.float32)
        act = (jax.nn.silu(gate_part) * up_part).astype(jnp.bfloat16)
        returned = jnp.dot(act, down_matrix, preferred_element_type=jnp.float32).astype(jnp.bfloat16)
        return returned.reshape(PROMPT_COUNT, CAP, D)
    served = lax.map(serve_expert, (jnp.arange(EXPERTS, dtype=jnp.int32), expert_gate, expert_up, expert_down))
    picked = served[flat_ids, prompt_ids, slot_index]
    picked = picked.reshape(PROMPT_COUNT, RESPONSE_COUNT, TOP, D).astype(jnp.float32)
    expert_sum = lax.optimization_barrier(jnp.sum(picked * routing_gates[:, :, :, None], axis=2))
    return (mid_rows.reshape(PROMPT_COUNT, RESPONSE_COUNT, D) + expert_sum).astype(jnp.bfloat16)
```

```python
import functools

import jax
import jax.numpy as jnp
import numpy as np
from jax import lax
from jax.experimental import pallas as pl
from jax.experimental.pallas import tpu as pltpu
from jax.sharding import PartitionSpec as P

MESH = pl.DeviceIdType.MESH
BF, F32 = jnp.bfloat16, jnp.float32

D = 2048
HS = 128
GROUPS = 4
HPG = 8
ROWS = 32
T = 4096
FE = 768
CAP = 5
SLOTS = 16 * CAP
QR = ROWS * HPG
TC = 1024
NC = 4
FC = D // NC
YFIRST = (0,)
LOG2E = 1.4426950408889634


def where_am_i():
    r, x, col = lax.axis_index("role"), lax.axis_index("row"), lax.axis_index("col")
    return r, x, lax.div(col, 4), lax.rem(col, 4)


def up(v, j):
    return lax.rem(v + j, 4)


def remote(src, dst, send, recv, dev):
    return pltpu.make_async_remote_copy(
        src_ref=src, dst_ref=dst, send_sem=send, recv_sem=recv, device_id=dev, device_id_type=MESH
    )


def attention_body(q_ref, k_hbm, v_hbm, nk_ref, nv_ref, hid_ref, w_hbm, gain_ref, mid_ref, normed_ref,
                   kv, vv, wv, sc, a_out, a_in, p_out, p_in, ksem, vsem, wsem, as_sem, ar_sem, ps_sem, pr_sem):
    r, x, z, y = where_am_i()
    col = z * 4 + y
    loads = []
    for j in range(GROUPS):
        g = up(x, 1 + j)
        cols = pl.ds(pl.multiple_of(g * HS, HS), HS)
        ck = pltpu.make_async_copy(k_hbm.at[:, cols], kv.at[j], ksem.at[j])
        cv = pltpu.make_async_copy(v_hbm.at[:, cols], vv.at[j], vsem.at[j])
        ck.start()
        cv.start()
        loads.append((ck, cv))
        if j == 0:
            cw = pltpu.make_async_copy(w_hbm, wv, wsem)
            cw.start()

    barrier = pltpu.get_barrier_semaphore()
    for j in range(1, 4):
        pl.semaphore_signal(barrier, inc=1, device_id=(r, up(x, j), col), device_id_type=MESH)
    pl.semaphore_wait(barrier, 3)

    scale = HS ** -0.5 * LOG2E
    outs, backs = [], []

    def serve(j):
        outs[j].wait_recv()
        if j == 0:
            cw.wait()
        p_out[j] = jnp.dot(a_in[j], wv[...], preferred_element_type=F32).astype(BF)
        back = remote(p_out.at[j], p_in.at[j], ps_sem.at[j], pr_sem.at[j], (r, up(x, 3 - j), col))
        back.start()
        backs.append(back)

    for j in range(GROUPS):
        g = up(x, 1 + j)
        q = jnp.concatenate(
            [q_ref[:, pl.ds(pl.multiple_of(g * (HPG * HS) + h * HS, HS), HS)] for h in range(HPG)], axis=0
        )
        gcols = pl.ds(pl.multiple_of(g * HS, HS), HS)
        own_k = jnp.concatenate([nk_ref[:, gcols]] * HPG, axis=0)
        own_v = jnp.concatenate([nv_ref[:, gcols]] * HPG, axis=0)
        own = jnp.sum(q.astype(F32) * own_k.astype(F32), axis=1, keepdims=True)
        loads[j][0].wait()

        def qk(i, m):
            at = pl.ds(pl.multiple_of(i * TC, TC), TC)
            s = lax.dot_general(q, kv[j, at, :], (((1,), (1,)), ((), ())), preferred_element_type=F32)
            sc[:, at] = s
            for b in range(TC // HS):
                m = jnp.maximum(m, s[:, b * HS:(b + 1) * HS])
            return m

        m = lax.fori_loop(0, T // TC, qk, jnp.full((QR, HS), -jnp.inf, F32))
        top = jnp.maximum(jnp.max(m, axis=1, keepdims=True), own)
        if j >= 1:
            serve(j - 1)
        loads[j][1].wait()

        def pv(i, carry):
            acc, den = carry
            at = pl.ds(pl.multiple_of(i * TC, TC), TC)
            e = jnp.exp2((sc[:, at] - top) * scale)
            for b in range(TC // HS):
                den = den + e[:, b * HS:(b + 1) * HS]
            acc = acc + jnp.dot(e.astype(BF), vv[j, at, :], preferred_element_type=F32)
            return acc, den

        zero = jnp.zeros((QR, HS), F32)
        acc, den = lax.fori_loop(0, T // TC, pv, (zero, zero))
        own_e = jnp.exp2((own - top) * scale)
        total = jnp.sum(den, axis=1, keepdims=True) + own_e
        att = ((acc + own_e * own_v.astype(F32)) / total).astype(BF)
        for h in range(HPG):
            a_out[j, :, h * HS:(h + 1) * HS] = att[h * ROWS:(h + 1) * ROWS]
        if j < 3:
            cp = remote(a_out.at[j], a_in.at[j], as_sem.at[j], ar_sem.at[j], (r, g, col))
            cp.start()
            outs.append(cp)

    mid = hid_ref[...].astype(F32) + jnp.dot(a_out[3], wv[...], preferred_element_type=F32)
    for j in range(3):
        backs[j].wait_recv()
        mid = mid + p_in[j].astype(F32)
    mid_ref[...] = mid
    ms = jnp.mean(mid * mid, axis=1, keepdims=True)
    normed_ref[...] = (mid * lax.rsqrt(ms + 1e-6) * gain_ref[...]).astype(BF)
    for j in range(3):
        outs[j].wait_send()
        backs[j].wait_send()


ATT_SCRATCH = [
    pltpu.VMEM((GROUPS, T, HS), BF),
    pltpu.VMEM((GROUPS, T, HS), BF),
    pltpu.VMEM((HPG * HS, D), BF),
    pltpu.VMEM((QR, T), F32),
    pltpu.VMEM((GROUPS, ROWS, HPG * HS), BF),
    pltpu.VMEM((3, ROWS, HPG * HS), BF),
    pltpu.VMEM((3, ROWS, D), BF),
    pltpu.VMEM((3, ROWS, D), BF),
    pltpu.SemaphoreType.DMA((GROUPS,)),
    pltpu.SemaphoreType.DMA((GROUPS,)),
    pltpu.SemaphoreType.DMA,
    pltpu.SemaphoreType.DMA((3,)),
    pltpu.SemaphoreType.DMA((3,)),
    pltpu.SemaphoreType.DMA((3,)),
    pltpu.SemaphoreType.DMA((3,)),
]


def attention_call(q, k, v, nk, nv, hid, w, gain):
    vmem, hbm = pl.BlockSpec(memory_space=pltpu.VMEM), pl.BlockSpec(memory_space=pl.ANY)
    return pl.pallas_call(
        attention_body,
        out_shape=(jax.ShapeDtypeStruct((ROWS, D), F32), jax.ShapeDtypeStruct((ROWS, D), BF)),
        in_specs=[vmem, hbm, hbm, vmem, vmem, vmem, hbm, vmem],
        out_specs=(vmem, vmem),
        scratch_shapes=ATT_SCRATCH,
        compiler_params=pltpu.CompilerParams(
            collective_id=0, has_side_effects=True, vmem_limit_bytes=56 * 2**20
        ),
        name="attention",
    )(q, k, v, nk, nv, hid, w, gain)


def table_constants():
    j = np.arange(8 * SLOTS)
    d, p, s = j // SLOTS, (j % SLOTS) // CAP, j % CAP
    rows = np.zeros((8, 8 * SLOTS), np.int32)
    rows[0], rows[1], rows[2], rows[3] = d // 4, d % 4, p, s
    i = np.arange(SLOTS)
    want = np.where((i // CAP)[:, None] == (np.arange(512) // ROWS)[None, :], (i % CAP)[:, None], -7)
    return rows, want.astype(np.float32)


def expert_body(normed_ref, mid_ref, ids_ref, gates_ref, rows_ref, want_ref, wg_hbm, wu_hbm, wd_hbm, out_ref,
                gath, tab, pack, block, wg, wu, wd, gacc, uacc, act, res, ret, part, part_in, half, half_in,
                sel, comb, wsem, ts, tr, s1s, s1r, s2s, s2r, ls, lr, locs, bs, br, h1s, h1r, h2s, h2r):
    r, x, z, y = where_am_i()
    a = jnp.where(r == 0, z, x)
    l = jnp.where(r == 0, x, z)

    def at(role, l_, a_, y_):
        xx = jnp.where(r == 0, l_, a_)
        zz = jnp.where(r == 0, a_, l_)
        return (role, xx, zz * 4 + y_)

    wcopies = [
        pltpu.make_async_copy(wg_hbm, wg, wsem.at[0]),
        pltpu.make_async_copy(wu_hbm, wu, wsem.at[1]),
        pltpu.make_async_copy(wd_hbm, wd, wsem.at[2]),
    ]
    for cp in wcopies:
        cp.start()

    barrier = pltpu.get_barrier_semaphore()
    partners = []
    for j in range(1, 4):
        partners += [at(r, up(l, j), a, y), at(r, l, up(a, j), y), at(r, l, a, up(y, j)),
                     at(1 - r, up(l, j), a, y), at(1 - r, l, up(a, j), y)]
    partners.append(at(1 - r, l, a, y))
    for dev in partners:
        pl.semaphore_signal(barrier, inc=1, device_id=dev, device_id_type=MESH)
    pl.semaphore_wait(barrier, len(partners))

    lane = lax.broadcasted_iota(jnp.int32, (ROWS, 128), 1)
    named = jnp.zeros((ROWS, 128), F32)
    gate = jnp.zeros((ROWS, 128), F32)
    for k in range(8):
        hit = ids_ref[:, k:k + 1] == lane
        named = jnp.where(hit, 1.0, named)
        gate = jnp.where(hit, gates_ref[:, k:k + 1], gate)
    before = lax.broadcasted_iota(jnp.int32, (ROWS, ROWS), 0) > lax.broadcasted_iota(jnp.int32, (ROWS, ROWS), 1)
    rank = jnp.dot(jnp.where(before, 1.0, 0.0).astype(BF), named.astype(BF), preferred_element_type=F32)
    tab[y, a, :, 0:128] = jnp.where(named > 0, rank, -1.0).astype(BF)
    tab[y, a, :, 128:256] = gate.astype(BF)

    pend = []

    def go(cp):
        cp.start()
        pend.append(cp)
        return cp

    t1 = [go(remote(tab.at[y, a], tab.at[y, a], ts.at[j - 1], tr.at[j - 1], at(r, l, up(a, j), y))) for j in range(1, 4)]

    first = []
    for c in range(NC):
        gath[c, y, a] = normed_ref[:, c * FC:(c + 1) * FC]
        cps = []
        for j in range(1, 4):
            dev = at(r, l, a, up(y, j)) if c in YFIRST else at(r, l, up(a, j), y)
            cps.append(go(remote(gath.at[c, y, a], gath.at[c, y, a], s1s.at[c, j - 1], s1r.at[c, j - 1], dev)))
        first.append(cps)

    for cp in t1:
        cp.wait_recv()
    t2 = [go(remote(tab.at[y], tab.at[y], ts.at[j + 2], tr.at[j + 2], at(r, l, a, up(y, j)))) for j in range(1, 4)]

    second = []
    for c in range(NC):
        for cp in first[c]:
            cp.wait_recv()
        cps = []
        for j in range(1, 4):
            if c in YFIRST:
                ref, dev = gath.at[c, :, a], at(r, l, up(a, j), y)
            else:
                ref, dev = gath.at[c, y], at(r, l, a, up(y, j))
            cps.append(go(remote(ref, ref, s2s.at[c, j - 1], s2r.at[c, j - 1], dev)))
        second.append(cps)

    for cp in t2:
        cp.wait_recv()
    step = jnp.where(r == 0, 16, 4)
    base = jnp.where(r == 0, z * 4 + y, x * 16 + y)
    ranks = tab[:, :, :, 0:128].reshape(512, 128)
    gates = tab[:, :, :, 128:256].reshape(512, 128)
    d8 = lax.broadcasted_iota(jnp.int32, (8, 128), 0)
    e8 = lax.broadcasted_iota(jnp.int32, (8, 128), 1)
    pick = jnp.where(e8 == (d8 >> 2) * 64 + (d8 & 3) * step + base, 1.0, 0.0).astype(BF)
    by_lane = lax.dot_general(pick, ranks, (((1,), (1,)), ((), ())), preferred_element_type=F32)
    for d in range(8):
        sel[d * SLOTS:(d + 1) * SLOTS, :] = jnp.where(want_ref[...] == by_lane[d:d + 1, :], 1.0, 0.0).astype(BF)
    e_of = rows_ref[0:1, :] * 64 + rows_ref[1:2, :] * step + base
    spread = jnp.where(lax.broadcasted_iota(jnp.int32, (128, 8 * SLOTS), 0) == e_of, 1.0, 0.0).astype(BF)
    rank_at = jnp.dot(ranks, spread, preferred_element_type=F32)
    gate_at = jnp.dot(gates, spread, preferred_element_type=F32)
    prompt = lax.broadcasted_iota(jnp.int32, (512, 8 * SLOTS), 0) >> 5
    mine = (prompt == rows_ref[2:3, :]) & (rank_at == rows_ref[3:4, :].astype(F32))
    comb[...] = jnp.where(mine, gate_at, 0.0).astype(BF)

    src = r * 4 + l
    third, local = [], []

    def send_slots(c):
        for cp in second[c]:
            cp.wait_recv()
        rows = gath[c].reshape(512, FC)
        pack[c] = jnp.dot(sel[...], rows, preferred_element_type=F32).astype(BF).reshape(8, SLOTS, FC)
        cps = []
        for j in range(7):
            if j < 3:
                d, dev = r * 4 + up(l, j + 1), at(r, up(l, j + 1), a, y)
            else:
                d, dev = (1 - r) * 4 + up(l, j - 3), at(1 - r, up(l, j - 3), a, y)
            cps.append(go(remote(pack.at[c, d], block.at[c, src], ls.at[c, j], lr.at[c, j], dev)))
        third.append(cps)
        own = pltpu.make_async_copy(pack.at[c, src], block.at[c, src], locs.at[0, c])
        own.start()
        local.append(own)

    def gate_up(c):
        for cp in third[c]:
            cp.wait_recv()
        local[c].wait()
        if c == 0:
            wcopies[0].wait()
            wcopies[1].wait()
        rows = block[c].reshape(8 * SLOTS, FC)
        at_f = slice(c * FC, (c + 1) * FC)
        gp = jnp.dot(rows, wg[at_f, :], preferred_element_type=F32)
        upp = jnp.dot(rows, wu[at_f, :], preferred_element_type=F32)
        if c == 0:
            gacc[...] = gp
            uacc[...] = upp
        elif c < NC - 1:
            gacc[...] += gp
            uacc[...] += upp
        else:
            gp = gp + gacc[...]
            act[...] = (gp * jax.nn.sigmoid(gp) * (upp + uacc[...])).astype(BF)

    for c in range(NC):
        send_slots(c)
        if c >= 1:
            gate_up(c - 1)
    gate_up(NC - 1)

    wcopies[2].wait()
    back, b_local, h1, h2 = [], [], [], []

    def down(c):
        o = jnp.dot(act[...], wd[:, c * FC:(c + 1) * FC], preferred_element_type=F32).astype(BF)
        res[c] = o.reshape(8, SLOTS, FC)
        cps = []
        for j in range(7):
            if j < 3:
                s, d, dev = r * 4 + up(l, j + 1), r * 4 + l, at(r, up(l, j + 1), a, y)
            else:
                s, d, dev = (1 - r) * 4 + up(a, j - 3), r * 4 + a, at(1 - r, l, up(a, j - 3), y)
            cps.append(go(remote(res.at[c, s], ret.at[c, d], bs.at[c, j], br.at[c, j], dev)))
        back.append(cps)
        own = pltpu.make_async_copy(res.at[c, src], ret.at[c, src], locs.at[1, c])
        own.start()
        b_local.append(own)

    def combine(c):
        for cp in back[c]:
            cp.wait_recv()
        b_local[c].wait()
        o = jnp.dot(comb[...], ret[c].reshape(8 * SLOTS, FC), preferred_element_type=F32).astype(BF)
        part[c] = o.reshape(4, 4, ROWS, FC)
        cps = []
        for j in range(1, 4):
            if c in YFIRST:
                ref, dev = part.at[c, :, up(a, j)], at(r, l, up(a, j), y)
            else:
                ref, dev = part.at[c, up(y, j)], at(r, l, a, up(y, j))
            cps.append(go(remote(ref, part_in.at[c, j - 1], h1s.at[c, j - 1], h1r.at[c, j - 1], dev)))
        h1.append(cps)

    def sum_one(c):
        for cp in h1[c]:
            cp.wait_recv()
        own = part[c, :, a] if c in YFIRST else part[c, y]
        o = own.astype(F32)
        for j in range(3):
            o = o + part_in[c, j].astype(F32)
        half[c] = o.astype(BF)
        cps = []
        for j in range(1, 4):
            if c in YFIRST:
                q, dev = up(y, j), at(r, l, a, up(y, j))
            else:
                q, dev = up(a, j), at(r, l, up(a, j), y)
            cps.append(go(remote(half.at[c, q], half_in.at[c, j - 1], h2s.at[c, j - 1], h2r.at[c, j - 1], dev)))
        h2.append(cps)

    def sum_two(c):
        for cp in h2[c]:
            cp.wait_recv()
        o = half[c, y if c in YFIRST else a].astype(F32)
        for j in range(3):
            o = o + half_in[c, j].astype(F32)
        at_f = slice(c * FC, (c + 1) * FC)
        out_ref[:, at_f] = (mid_ref[:, at_f] + o).astype(BF)

    for t in range(NC + 3):
        if t < NC:
            down(t)
        if 0 <= t - 1 < NC:
            combine(t - 1)
        if 0 <= t - 2 < NC:
            sum_one(t - 2)
        if 0 <= t - 3 < NC:
            sum_two(t - 3)
    for cp in pend:
        cp.wait_send()


EXP_SCRATCH = [
    pltpu.VMEM((NC, 4, 4, ROWS, FC), BF),
    pltpu.VMEM((4, 4, ROWS, 256), BF),
    pltpu.VMEM((NC, 8, SLOTS, FC), BF),
    pltpu.VMEM((NC, 8, SLOTS, FC), BF),
    pltpu.VMEM((D, FE), BF),
    pltpu.VMEM((D, FE), BF),
    pltpu.VMEM((FE, D), BF),
    pltpu.VMEM((8 * SLOTS, FE), F32),
    pltpu.VMEM((8 * SLOTS, FE), F32),
    pltpu.VMEM((8 * SLOTS, FE), BF),
    pltpu.VMEM((NC, 8, SLOTS, FC), BF),
    pltpu.VMEM((NC, 8, SLOTS, FC), BF),
    pltpu.VMEM((NC, 4, 4, ROWS, FC), BF),
    pltpu.VMEM((NC, 3, 4, ROWS, FC), BF),
    pltpu.VMEM((NC, 4, ROWS, FC), BF),
    pltpu.VMEM((NC, 3, ROWS, FC), BF),
    pltpu.VMEM((8 * SLOTS, 512), BF),
    pltpu.VMEM((512, 8 * SLOTS), BF),
    pltpu.SemaphoreType.DMA((3,)),
    pltpu.SemaphoreType.DMA((6,)),
    pltpu.SemaphoreType.DMA((6,)),
    pltpu.SemaphoreType.DMA((NC, 3)),
    pltpu.SemaphoreType.DMA((NC, 3)),
    pltpu.SemaphoreType.DMA((NC, 3)),
    pltpu.SemaphoreType.DMA((NC, 3)),
    pltpu.SemaphoreType.DMA((NC, 7)),
    pltpu.SemaphoreType.DMA((NC, 7)),
    pltpu.SemaphoreType.DMA((2, NC)),
    pltpu.SemaphoreType.DMA((NC, 7)),
    pltpu.SemaphoreType.DMA((NC, 7)),
    pltpu.SemaphoreType.DMA((NC, 3)),
    pltpu.SemaphoreType.DMA((NC, 3)),
    pltpu.SemaphoreType.DMA((NC, 3)),
    pltpu.SemaphoreType.DMA((NC, 3)),
]


def expert_call(normed, mid, ids, gates, wg, wu, wd):
    vmem, hbm = pl.BlockSpec(memory_space=pltpu.VMEM), pl.BlockSpec(memory_space=pl.ANY)
    rows, want = table_constants()
    return pl.pallas_call(
        expert_body,
        out_shape=jax.ShapeDtypeStruct((ROWS, D), BF),
        in_specs=[vmem] * 6 + [hbm] * 3,
        out_specs=vmem,
        scratch_shapes=EXP_SCRATCH,
        compiler_params=pltpu.CompilerParams(
            collective_id=1, has_side_effects=True, vmem_limit_bytes=56 * 2**20
        ),
        name="experts",
    )(normed, mid, ids, gates, jnp.asarray(rows), jnp.asarray(want), wg, wu, wd)


def per_device(queries, cache_keys, prompt_value_cache, new_keys, fresh_token_values, hidden, out_weight, norm_gain,
               expert_gate, expert_up, expert_down, expert_ids, routing_gates):
    mid, normed = attention_call(
        queries[0], cache_keys[0], prompt_value_cache[0], new_keys[0], fresh_token_values[0], hidden[0], out_weight,
        norm_gain[None, :],
    )
    out = expert_call(normed, mid, expert_ids[0], routing_gates[0], expert_gate[0], expert_up[0], expert_down[0])
    return out[None]


def solution(mesh):
    split = P(("role", "row", "col"), None, None)
    return jax.shard_map(
        per_device,
        mesh=mesh,
        in_specs=(split,) * 6 + (P("row", None), P()) + (split,) * 5,
        out_specs=split,
        check_vma=False,
    )
```

```python
import jax
import jax.numpy as jnp
from jax import lax
from jax.experimental import pallas as pl
from jax.experimental.pallas import tpu as pltpu
from jax.sharding import PartitionSpec as P

MESH = pl.DeviceIdType.MESH
BF, F32 = jnp.bfloat16, jnp.float32

D = 2048
HS = 128
GROUPS = 4
HPG = 8
ROWS = 32
T = 4096
FE = 768
CAP = 5
SLOTS = 16 * CAP
QR = ROWS * HPG
TC = 1024
NC = 4
FC = D // NC
YFIRST = (0,)
THROTTLE = True
VMEM_LIMIT = 60 * 2**20
LOG2E = 1.4426950408889634


def where_am_i():
    r, x, col = lax.axis_index("role"), lax.axis_index("row"), lax.axis_index("col")
    return r, x, lax.div(col, 4), lax.rem(col, 4)


def up(v, j):
    return lax.rem(v + j, 4)


def remote(src, dst, send, recv, dev):
    return pltpu.make_async_remote_copy(
        src_ref=src, dst_ref=dst, send_sem=send, recv_sem=recv, device_id=dev, device_id_type=MESH
    )


def layer_body(q_hbm, k_hbm, v_hbm, nk_hbm, nv_hbm, hid_hbm, w_hbm, gain_ref, ids_ref, gates_ref, wg_hbm, wu_hbm,
               wd_hbm, out_ref,
               qv, nkv, nvv, hidv, kv, vv, wv, sc, a_out, a_in, p_out, p_in, mid_ref,
               gath, tab, pack, block, wg, wu, wd, gacc, uacc, act, res, ret, part, part_in, half, half_in, sel, comb,
               insem, ksem, vsem, wsem, as_sem, ar_sem, ps_sem, pr_sem,
               ts, tr, s1s, s1r, s2s, s2r, ls, lr, locs, bs, br, h1s, h1r, h2s, h2r):
    r, x, z, y = where_am_i()
    col = z * 4 + y
    a = jnp.where(r == 0, z, x)
    l = jnp.where(r == 0, x, z)

    def at(role, l_, a_, y_):
        xx = jnp.where(r == 0, l_, a_)
        zz = jnp.where(r == 0, a_, l_)
        return (role, xx, zz * 4 + y_)

    def load(src, dst, sem):
        return pltpu.make_async_copy(src, dst, sem)

    kloads, vloads = [], []
    for j in range(GROUPS):
        cols = pl.ds(pl.multiple_of(up(x, 1 + j) * HS, HS), HS)
        kloads.append(load(k_hbm.at[:, cols], kv.at[j], ksem.at[j]))
        vloads.append(load(v_hbm.at[:, cols], vv.at[j], vsem.at[j]))
    ins = [load(q_hbm, qv, insem.at[0]), load(nk_hbm, nkv, insem.at[1]), load(nv_hbm, nvv, insem.at[2]),
           load(hid_hbm, hidv, insem.at[3])]
    cw = load(w_hbm, wv, wsem.at[3])
    wcopies = [load(wg_hbm, wg, wsem.at[0]), load(wu_hbm, wu, wsem.at[1]), load(wd_hbm, wd, wsem.at[2])]
    for cp in ins:
        cp.start()
    kloads[0].start()
    vloads[0].start()

    barrier = pltpu.get_barrier_semaphore()
    partners = [at(1 - r, l, a, y)]
    for j in range(1, 4):
        partners += [at(r, up(l, j), a, y), at(r, l, up(a, j), y), at(r, l, a, up(y, j)),
                     at(1 - r, up(l, j), a, y), at(1 - r, l, up(a, j), y)]
    for dev in partners:
        pl.semaphore_signal(barrier, inc=1, device_id=dev, device_id_type=MESH)

    lane = lax.broadcasted_iota(jnp.int32, (ROWS, 128), 1)
    named = jnp.zeros((ROWS, 128), F32)
    gate = jnp.zeros((ROWS, 128), F32)
    for k in range(8):
        hit = ids_ref[:, k:k + 1] == lane
        named = jnp.where(hit, 1.0, named)
        gate = jnp.where(hit, gates_ref[:, k:k + 1], gate)
    before = lax.broadcasted_iota(jnp.int32, (ROWS, ROWS), 0) > lax.broadcasted_iota(jnp.int32, (ROWS, ROWS), 1)
    rank = jnp.dot(jnp.where(before, 1.0, 0.0).astype(BF), named.astype(BF), preferred_element_type=F32)
    tab[y, a, :, 0:128] = jnp.where(named > 0, rank, -1.0).astype(BF)
    tab[y, a, :, 128:256] = gate.astype(BF)

    pl.semaphore_wait(barrier, len(partners))

    pend = []

    def go(cp):
        cp.start()
        pend.append(cp)
        return cp

    t1 = [go(remote(tab.at[y, a], tab.at[y, a], ts.at[j - 1], tr.at[j - 1], at(r, l, up(a, j), y))) for j in range(1, 4)]
    t2 = []

    scale = HS ** -0.5 * LOG2E
    outs, backs = [], []

    def serve(j):
        outs[j].wait_recv()
        if j == 0:
            cw.wait()
        p_out[j] = jnp.dot(a_in[j], wv[...], preferred_element_type=F32).astype(BF)
        backs.append(go(remote(p_out.at[j], p_in.at[j], ps_sem.at[j], pr_sem.at[j], (r, up(x, 3 - j), col))))

    for j in range(GROUPS):
        g = up(x, 1 + j)
        if j == 0:
            for cp in ins[:3]:
                cp.wait()
        q = jnp.concatenate(
            [qv[:, pl.ds(pl.multiple_of(g * (HPG * HS) + h * HS, HS), HS)] for h in range(HPG)], axis=0
        )
        gcols = pl.ds(pl.multiple_of(g * HS, HS), HS)
        own_k = jnp.concatenate([nkv[:, gcols]] * HPG, axis=0)
        own_v = jnp.concatenate([nvv[:, gcols]] * HPG, axis=0)
        own = jnp.sum(q.astype(F32) * own_k.astype(F32), axis=1, keepdims=True)
        kloads[j].wait()
        if j + 1 < GROUPS:
            kloads[j + 1].start()
            vloads[j + 1].start()
            if j == 0:
                cw.start()
        else:
            for cp in wcopies:
                cp.start()

        def qk(i, m):
            rows = pl.ds(pl.multiple_of(i * TC, TC), TC)
            s = lax.dot_general(q, kv[j, rows, :], (((1,), (1,)), ((), ())), preferred_element_type=F32)
            sc[:, rows] = s
            for b in range(TC // HS):
                m = jnp.maximum(m, s[:, b * HS:(b + 1) * HS])
            return m

        m = lax.fori_loop(0, T // TC, qk, jnp.full((QR, HS), -jnp.inf, F32))
        top = jnp.maximum(jnp.max(m, axis=1, keepdims=True), own)
        vloads[j].wait()

        def pv(i, carry):
            acc, den = carry
            rows = pl.ds(pl.multiple_of(i * TC, TC), TC)
            e = jnp.exp2((sc[:, rows] - top) * scale)
            for b in range(TC // HS):
                den = den + e[:, b * HS:(b + 1) * HS]
            acc = acc + jnp.dot(e.astype(BF), vv[j, rows, :], preferred_element_type=F32)
            return acc, den

        zero = jnp.zeros((QR, HS), F32)
        acc, den = lax.fori_loop(0, T // TC, pv, (zero, zero))
        own_e = jnp.exp2((own - top) * scale)
        total = jnp.sum(den, axis=1, keepdims=True) + own_e
        att = ((acc + own_e * own_v.astype(F32)) / total).astype(BF)
        for h in range(HPG):
            a_out[j, :, h * HS:(h + 1) * HS] = att[h * ROWS:(h + 1) * ROWS]
        if j < 3:
            outs.append(go(remote(a_out.at[j], a_in.at[j], as_sem.at[j], ar_sem.at[j], (r, g, col))))
        if j == 0:
            for cp in t1:
                cp.wait_recv()
            for i in range(1, 4):
                t2.append(go(remote(tab.at[y], tab.at[y], ts.at[i + 2], tr.at[i + 2], at(r, l, a, up(y, i)))))
        if j >= 1:
            serve(j - 1)

    ins[3].wait()
    mid = hidv[...].astype(F32) + jnp.dot(a_out[3], wv[...], preferred_element_type=F32)
    mid_ref[...] = mid

    for cp in t2:
        cp.wait_recv()
    step = jnp.where(r == 0, 16, 4)
    base = jnp.where(r == 0, z * 4 + y, x * 16 + y)
    ranks = tab[:, :, :, 0:128].reshape(512, 128)
    gates = tab[:, :, :, 128:256].reshape(512, 128)
    d8 = lax.broadcasted_iota(jnp.int32, (8, 128), 0)
    e8 = lax.broadcasted_iota(jnp.int32, (8, 128), 1)
    pick = jnp.where(e8 == (d8 >> 2) * 64 + (d8 & 3) * step + base, 1.0, 0.0).astype(BF)
    by_lane = lax.dot_general(pick, ranks, (((1,), (1,)), ((), ())), preferred_element_type=F32)
    slot = lax.broadcasted_iota(jnp.int32, (SLOTS, 512), 0)
    its_prompt = (slot * 205) >> 10
    same = its_prompt == (lax.broadcasted_iota(jnp.int32, (SLOTS, 512), 1) >> 5)
    want = jnp.where(same, slot - its_prompt * CAP, -7).astype(F32)
    for d in range(8):
        sel[d * SLOTS:(d + 1) * SLOTS, :] = jnp.where(want == by_lane[d:d + 1, :], 1.0, 0.0).astype(BF)
    lane_j = lax.broadcasted_iota(jnp.int32, (1, 8 * SLOTS), 1)
    d_of = (lane_j * 205) >> 14
    rem = lane_j - d_of * SLOTS
    p_of = (rem * 205) >> 10
    s_of = (rem - p_of * CAP).astype(F32)
    e_of = (d_of >> 2) * 64 + (d_of & 3) * step + base
    spread = jnp.where(lax.broadcasted_iota(jnp.int32, (128, 8 * SLOTS), 0) == e_of, 1.0, 0.0).astype(BF)
    rank_at = jnp.dot(ranks, spread, preferred_element_type=F32)
    gate_at = jnp.dot(gates, spread, preferred_element_type=F32)
    prompt = lax.broadcasted_iota(jnp.int32, (512, 8 * SLOTS), 0) >> 5
    comb[...] = jnp.where((prompt == p_of) & (rank_at == s_of), gate_at, 0.0).astype(BF)

    for j in range(3):
        backs[j].wait_recv()
    mid = mid_ref[...]
    for j in range(3):
        mid = mid + p_in[j].astype(F32)
    mid_ref[...] = mid
    ms = jnp.mean(mid * mid, axis=1, keepdims=True)
    normed = (mid * lax.rsqrt(ms + 1e-6) * gain_ref[...]).astype(BF)

    first = []
    for c in range(NC):
        gath[c, y, a] = normed[:, c * FC:(c + 1) * FC]
        cps = []
        for j in range(1, 4):
            dev = at(r, l, a, up(y, j)) if c in YFIRST else at(r, l, up(a, j), y)
            cps.append(go(remote(gath.at[c, y, a], gath.at[c, y, a], s1s.at[c, j - 1], s1r.at[c, j - 1], dev)))
        first.append(cps)

    second = [None] * NC

    def spread_second(c):
        for cp in first[c]:
            cp.wait_recv()
        cps = []
        for j in range(1, 4):
            if c in YFIRST:
                ref, dev = gath.at[c, :, a], at(r, l, up(a, j), y)
            else:
                ref, dev = gath.at[c, y], at(r, l, a, up(y, j))
            cps.append(go(remote(ref, ref, s2s.at[c, j - 1], s2r.at[c, j - 1], dev)))
        second[c] = cps

    src = r * 4 + l
    third, local = [None] * NC, [None] * NC

    def send_slots(c):
        for cp in second[c]:
            cp.wait_recv()
        rows = gath[c].reshape(512, FC)
        pack[c] = jnp.dot(sel[...], rows, preferred_element_type=F32).astype(BF).reshape(8, SLOTS, FC)
        cps = []
        for j in range(7):
            if j < 3:
                d, dev = r * 4 + up(l, j + 1), at(r, up(l, j + 1), a, y)
            else:
                d, dev = (1 - r) * 4 + up(l, j - 3), at(1 - r, up(l, j - 3), a, y)
            cps.append(go(remote(pack.at[c, d], block.at[c, src], ls.at[c, j], lr.at[c, j], dev)))
        third[c] = cps
        own = pltpu.make_async_copy(pack.at[c, src], block.at[c, src], locs.at[0, c])
        own.start()
        local[c] = own

    def gate_up(c, begin, end):
        for cp in third[c]:
            cp.wait_recv()
        local[c].wait()
        if begin:
            wcopies[0].wait()
            wcopies[1].wait()
        rows = block[c].reshape(8 * SLOTS, FC)
        at_f = slice(c * FC, (c + 1) * FC)
        gp = jnp.dot(rows, wg[at_f, :], preferred_element_type=F32)
        upp = jnp.dot(rows, wu[at_f, :], preferred_element_type=F32)
        if begin:
            gacc[...] = gp
            uacc[...] = upp
        elif not end:
            gacc[...] += gp
            uacc[...] += upp
        else:
            gp = gp + gacc[...]
            act[...] = (gp * jax.nn.sigmoid(gp) * (upp + uacc[...])).astype(BF)

    spread_second(1)
    spread_second(0)
    if not THROTTLE:
        spread_second(2)
        spread_second(3)
    for c in range(NC):
        send_slots(c)
        if THROTTLE and c + 2 < NC:
            for cp in second[c + 1]:
                cp.wait_send()
                pend[:] = [p for p in pend if p is not cp]
            spread_second(c + 2)
        if c >= 1:
            gate_up(c - 1, c == 1, False)
    gate_up(NC - 1, False, True)

    wcopies[2].wait()
    back, b_local, h1, h2 = [None] * NC, [None] * NC, [None] * NC, [None] * NC

    def down(c):
        o = jnp.dot(act[...], wd[:, c * FC:(c + 1) * FC], preferred_element_type=F32).astype(BF)
        res[c] = o.reshape(8, SLOTS, FC)
        cps = []
        for j in range(7):
            if j < 3:
                s, d, dev = r * 4 + up(l, j + 1), r * 4 + l, at(r, up(l, j + 1), a, y)
            else:
                s, d, dev = (1 - r) * 4 + up(a, j - 3), r * 4 + a, at(1 - r, l, up(a, j - 3), y)
            cps.append(go(remote(res.at[c, s], ret.at[c, d], bs.at[c, j], br.at[c, j], dev)))
        back[c] = cps
        own = pltpu.make_async_copy(res.at[c, src], ret.at[c, src], locs.at[1, c])
        own.start()
        b_local[c] = own

    def combine(c):
        for cp in back[c]:
            cp.wait_recv()
        b_local[c].wait()
        o = jnp.dot(comb[...], ret[c].reshape(8 * SLOTS, FC), preferred_element_type=F32).astype(BF)
        part[c] = o.reshape(4, 4, ROWS, FC)
        cps = []
        for j in range(1, 4):
            if c in YFIRST:
                ref, dev = part.at[c, :, up(a, j)], at(r, l, up(a, j), y)
            else:
                ref, dev = part.at[c, up(y, j)], at(r, l, a, up(y, j))
            cps.append(go(remote(ref, part_in.at[c, j - 1], h1s.at[c, j - 1], h1r.at[c, j - 1], dev)))
        h1[c] = cps

    def sum_one(c):
        for cp in h1[c]:
            cp.wait_recv()
        own = part[c, :, a] if c in YFIRST else part[c, y]
        o = own.astype(F32)
        for j in range(3):
            o = o + part_in[c, j].astype(F32)
        half[c] = o.astype(BF)
        cps = []
        for j in range(1, 4):
            if c in YFIRST:
                q, dev = up(y, j), at(r, l, a, up(y, j))
            else:
                q, dev = up(a, j), at(r, l, up(a, j), y)
            cps.append(go(remote(half.at[c, q], half_in.at[c, j - 1], h2s.at[c, j - 1], h2r.at[c, j - 1], dev)))
        h2[c] = cps

    def sum_two(c):
        for cp in h2[c]:
            cp.wait_recv()
        o = half[c, y if c in YFIRST else a].astype(F32)
        for j in range(3):
            o = o + half_in[c, j].astype(F32)
        at_f = slice(c * FC, (c + 1) * FC)
        out_ref[:, at_f] = (mid_ref[:, at_f] + o).astype(BF)

    order = list(range(1, NC)) + [0]
    stages = (down, combine, sum_one, sum_two)
    for t in range(NC + 3):
        for n, stage in enumerate(stages):
            if 0 <= t - n < NC:
                stage(order[t - n])
    for cp in pend:
        cp.wait_send()


def scratch():
    vm, dma = pltpu.VMEM, pltpu.SemaphoreType.DMA
    return [
        vm((ROWS, 4096), BF), vm((ROWS, 512), BF), vm((ROWS, 512), BF), vm((ROWS, D), BF),
        vm((GROUPS, T, HS), BF), vm((GROUPS, T, HS), BF), vm((HPG * HS, D), BF), vm((QR, T), F32),
        vm((GROUPS, ROWS, HPG * HS), BF), vm((3, ROWS, HPG * HS), BF), vm((3, ROWS, D), BF), vm((3, ROWS, D), BF),
        vm((ROWS, D), F32),
        vm((NC, 4, 4, ROWS, FC), BF), vm((4, 4, ROWS, 256), BF),
        vm((NC, 8, SLOTS, FC), BF), vm((NC, 8, SLOTS, FC), BF),
        vm((D, FE), BF), vm((D, FE), BF), vm((FE, D), BF),
        vm((8 * SLOTS, FE), F32), vm((8 * SLOTS, FE), F32), vm((8 * SLOTS, FE), BF),
        vm((NC, 8, SLOTS, FC), BF), vm((NC, 8, SLOTS, FC), BF),
        vm((NC, 4, 4, ROWS, FC), BF), vm((NC, 3, 4, ROWS, FC), BF), vm((NC, 4, ROWS, FC), BF), vm((NC, 3, ROWS, FC), BF),
        vm((8 * SLOTS, 512), BF), vm((512, 8 * SLOTS), BF),
        dma((4,)), dma((GROUPS,)), dma((GROUPS,)), dma((4,)), dma((3,)), dma((3,)), dma((3,)), dma((3,)),
        dma((6,)), dma((6,)), dma((NC, 3)), dma((NC, 3)), dma((NC, 3)), dma((NC, 3)), dma((NC, 7)), dma((NC, 7)),
        dma((2, NC)), dma((NC, 7)), dma((NC, 7)), dma((NC, 3)), dma((NC, 3)), dma((NC, 3)), dma((NC, 3)),
    ]


def layer_call(cid, *args):
    vmem, hbm = pl.BlockSpec(memory_space=pltpu.VMEM), pl.BlockSpec(memory_space=pl.ANY)
    return pl.pallas_call(
        layer_body,
        out_shape=jax.ShapeDtypeStruct((ROWS, D), BF),
        in_specs=[hbm] * 7 + [vmem] * 3 + [hbm] * 3,
        out_specs=vmem,
        scratch_shapes=scratch(),
        compiler_params=pltpu.CompilerParams(
            collective_id=cid, has_side_effects=True, vmem_limit_bytes=VMEM_LIMIT
        ),
        name="layer_%d" % cid,
    )(*args)


def per_device(queries, cache_keys, prompt_value_cache, new_keys, fresh_token_values, hidden, out_weight, norm_gain,
               expert_gate, expert_up, expert_down, expert_ids, routing_gates):
    out = layer_call(
        0, queries[0], cache_keys[0], prompt_value_cache[0], new_keys[0], fresh_token_values[0], hidden[0], out_weight,
        norm_gain[None, :], expert_ids[0], routing_gates[0], expert_gate[0], expert_up[0], expert_down[0],
    )
    return out[None]


def solution(mesh):
    split = P(("role", "row", "col"), None, None)
    return jax.shard_map(
        per_device,
        mesh=mesh,
        in_specs=(split,) * 6 + (P("row", None), P()) + (split,) * 5,
        out_specs=split,
        check_vma=False,
    )
```

```python
import jax
import jax.numpy as jnp
from jax import lax
from jax.experimental import pallas as pl
from jax.experimental.pallas import tpu as pltpu
from jax.sharding import PartitionSpec as P

MESH = pl.DeviceIdType.MESH
BF, F32 = jnp.bfloat16, jnp.float32

D = 2048
HS = 128
GROUPS = 4
HPG = 8
ROWS = 32
T = 4096
FE = 768
CAP = 5
SLOTS = 16 * CAP
QR = ROWS * HPG
TC = 1024
CHUNKS = ((0, 512, True), (512, 256, True), (768, 512, False), (1280, 512, False), (1792, 256, False))
TO_ORDER = (2, 0, 1, 3, 4)
SLOT_ORDER = (0, 1, 2, 3, 4)
BACK_ORDER = (4, 2, 3, 0, 1)
VMEM_LIMIT = 60 * 2**20
LOG2E = 1.4426950408889634


def where_am_i():
    r, x, col = lax.axis_index("role"), lax.axis_index("row"), lax.axis_index("col")
    return r, x, lax.div(col, 4), lax.rem(col, 4)


def up(v, j):
    return lax.rem(v + j, 4)


def remote(src, dst, send, recv, dev):
    return pltpu.make_async_remote_copy(
        src_ref=src, dst_ref=dst, send_sem=send, recv_sem=recv, device_id=dev, device_id_type=MESH
    )


def layer_body(q_hbm, k_hbm, v_hbm, nk_hbm, nv_hbm, hid_hbm, w_hbm, gain_ref, ids_ref, gates_ref, wg_hbm, wu_hbm,
               wd_hbm, out_ref,
               qv, nkv, nvv, hidv, kv, vv, wv, sc, a_out, a_in, p_out, p_in, mid_ref,
               tab, wg, wu, wd, gacc, uacc, act, sel, comb, gath, pack, block, res, ret, part, part_in, half, half_in,
               insem, ksem, vsem, wsem, as_sem, ar_sem, ps_sem, pr_sem,
               ts, tr, s1s, s1r, s2s, s2r, ls, lr, locs, bs, br, h1s, h1r, h2s, h2r):
    r, x, z, y = where_am_i()
    col = z * 4 + y
    a = jnp.where(r == 0, z, x)
    l = jnp.where(r == 0, x, z)

    def at(role, l_, a_, y_):
        xx = jnp.where(r == 0, l_, a_)
        zz = jnp.where(r == 0, a_, l_)
        return (role, xx, zz * 4 + y_)

    def load(src, dst, sem):
        return pltpu.make_async_copy(src, dst, sem)

    kloads, vloads = [], []
    for j in range(GROUPS):
        cols = pl.ds(pl.multiple_of(up(x, 1 + j) * HS, HS), HS)
        kloads.append(load(k_hbm.at[:, cols], kv.at[j], ksem.at[j]))
        vloads.append(load(v_hbm.at[:, cols], vv.at[j], vsem.at[j]))
    ins = [load(q_hbm, qv, insem.at[0]), load(nk_hbm, nkv, insem.at[1]), load(nv_hbm, nvv, insem.at[2]),
           load(hid_hbm, hidv, insem.at[3])]
    cw = load(w_hbm, wv, wsem.at[3])
    wcopies = [load(wg_hbm, wg, wsem.at[0]), load(wu_hbm, wu, wsem.at[1]), load(wd_hbm, wd, wsem.at[2])]
    for cp in ins:
        cp.start()
    kloads[0].start()
    vloads[0].start()
    kloads[1].start()

    barrier = pltpu.get_barrier_semaphore()
    partners = [at(1 - r, l, a, y)]
    for j in range(1, 4):
        partners += [at(r, up(l, j), a, y), at(r, l, up(a, j), y), at(r, l, a, up(y, j)),
                     at(1 - r, up(l, j), a, y), at(1 - r, l, up(a, j), y)]
    for dev in partners:
        pl.semaphore_signal(barrier, inc=1, device_id=dev, device_id_type=MESH)

    expert = lax.broadcasted_iota(jnp.int32, (128, ROWS), 0)
    named_t = jnp.zeros((128, ROWS), F32)
    gate_t = jnp.zeros((128, ROWS), F32)
    for k in range(8):
        hit = ids_ref[k:k + 1, :] == expert
        named_t = jnp.where(hit, 1.0, named_t)
        gate_t = jnp.where(hit, gates_ref[k:k + 1, :], gate_t)
    sq0 = lax.broadcasted_iota(jnp.int32, (ROWS, ROWS), 0)
    sq1 = lax.broadcasted_iota(jnp.int32, (ROWS, ROWS), 1)
    before = jnp.where(sq0 > sq1, 1.0, 0.0).astype(BF)
    same_row = jnp.where(sq0 == sq1, 1.0, 0.0).astype(BF)

    def rows_of(left, right):
        return lax.dot_general(left, right.astype(BF), (((1,), (1,)), ((), ())), preferred_element_type=F32)

    tab[y, a, :, 0:128] = jnp.where(rows_of(same_row, named_t) > 0, rows_of(before, named_t), -1.0).astype(BF)
    tab[y, a, :, 128:256] = rows_of(same_row, gate_t).astype(BF)

    pend = []

    def go(cp):
        cp.start()
        pend.append(cp)
        return cp

    t1, t2 = [], []

    scale = HS ** -0.5 * LOG2E
    outs, backs = [], []

    def serve(j):
        outs[j].wait_recv()
        if j == 0:
            cw.wait()
        p_out[j] = jnp.dot(a_in[j], wv[...], preferred_element_type=F32).astype(BF)
        backs.append(go(remote(p_out.at[j], p_in.at[j], ps_sem.at[j], pr_sem.at[j], (r, up(x, 3 - j), col))))

    def block_of(j):
        g = up(x, 1 + j)
        q = jnp.concatenate(
            [qv[:, pl.ds(pl.multiple_of(g * (HPG * HS) + h * HS, HS), HS)] for h in range(HPG)], axis=0
        )
        own_k = jnp.concatenate([nkv[:, pl.ds(pl.multiple_of(g * HS, HS), HS)]] * HPG, axis=0)
        return q, jnp.sum(q.astype(F32) * own_k.astype(F32), axis=1, keepdims=True)

    def keys_at(i):
        return pl.ds(pl.multiple_of(i * TC, TC), TC)

    def score(j, i, q, m):
        s = lax.dot_general(q, kv[j, keys_at(i), :], (((1,), (1,)), ((), ())), preferred_element_type=F32)
        sc[j % 2, :, keys_at(i)] = s
        for b in range(TC // HS):
            m = jnp.maximum(m, s[:, b * HS:(b + 1) * HS])
        return m

    def mix(j, i, top, acc, den):
        e = jnp.exp2((sc[j % 2, :, keys_at(i)] - top) * scale)
        for b in range(TC // HS):
            den = den + e[:, b * HS:(b + 1) * HS]
        return acc + jnp.dot(e.astype(BF), vv[j, keys_at(i), :], preferred_element_type=F32), den

    low, zero = jnp.full((QR, HS), -jnp.inf, F32), jnp.zeros((QR, HS), F32)
    for cp in ins[:3]:
        cp.wait()
    kloads[0].wait()
    q, own = block_of(0)
    m = lax.fori_loop(0, T // TC, lambda i, m: score(0, i, q, m), low)
    for j in range(GROUPS):
        g = up(x, 1 + j)
        own_v = jnp.concatenate([nvv[:, pl.ds(pl.multiple_of(g * HS, HS), HS)]] * HPG, axis=0)
        top = jnp.maximum(jnp.max(m, axis=1, keepdims=True), own)
        vloads[j].wait()
        if j + 2 < GROUPS:
            kloads[j + 2].start()
        if j + 1 < GROUPS:
            vloads[j + 1].start()
        if j == 0:
            cw.start()
        if j == 2:
            for cp in wcopies:
                cp.start()
        if j + 1 < GROUPS:
            kloads[j + 1].wait()
            q, next_own = block_of(j + 1)

            def both(i, carry):
                m, acc, den = carry
                m = score(j + 1, i, q, m)
                return m, *mix(j, i, top, acc, den)

            m, acc, den = lax.fori_loop(0, T // TC, both, (low, zero, zero))
        else:
            next_own = None
            acc, den = lax.fori_loop(0, T // TC, lambda i, carry: mix(j, i, top, *carry), (zero, zero))
        own_e = jnp.exp2((own - top) * scale)
        total = jnp.sum(den, axis=1, keepdims=True) + own_e
        att = ((acc + own_e * own_v.astype(F32)) / total).astype(BF)
        for h in range(HPG):
            a_out[j, :, h * HS:(h + 1) * HS] = att[h * ROWS:(h + 1) * ROWS]
        if j == 0:
            pl.semaphore_wait(barrier, len(partners))
        if j < 3:
            outs.append(go(remote(a_out.at[j], a_in.at[j], as_sem.at[j], ar_sem.at[j], (r, g, col))))
        if j == 0:
            for i in range(1, 4):
                t1.append(go(remote(tab.at[y, a], tab.at[y, a], ts.at[i - 1], tr.at[i - 1], at(r, l, up(a, i), y))))
        if j == 1:
            for cp in t1:
                cp.wait_recv()
            for i in range(1, 4):
                t2.append(go(remote(tab.at[y], tab.at[y], ts.at[i + 2], tr.at[i + 2], at(r, l, a, up(y, i)))))
        if j >= 1:
            serve(j - 1)
        own = next_own

    ins[3].wait()
    mid = hidv[...].astype(F32) + jnp.dot(a_out[3], wv[...], preferred_element_type=F32)
    mid_ref[...] = mid

    for cp in t2:
        cp.wait_recv()
    step = jnp.where(r == 0, 16, 4)
    base = jnp.where(r == 0, z * 4 + y, x * 16 + y)
    ranks = tab[:, :, :, 0:128].reshape(512, 128)
    gates = tab[:, :, :, 128:256].reshape(512, 128)
    d8 = lax.broadcasted_iota(jnp.int32, (8, 128), 0)
    e8 = lax.broadcasted_iota(jnp.int32, (8, 128), 1)
    pick = jnp.where(e8 == (d8 >> 2) * 64 + (d8 & 3) * step + base, 1.0, 0.0).astype(BF)
    by_lane = lax.dot_general(pick, ranks, (((1,), (1,)), ((), ())), preferred_element_type=F32)
    slot = lax.broadcasted_iota(jnp.int32, (SLOTS, 512), 0)
    its_prompt = (slot * 205) >> 10
    same = its_prompt == (lax.broadcasted_iota(jnp.int32, (SLOTS, 512), 1) >> 5)
    want = jnp.where(same, slot - its_prompt * CAP, -7).astype(F32)
    for d in range(8):
        sel[d * SLOTS:(d + 1) * SLOTS, :] = jnp.where(want == by_lane[d:d + 1, :], 1.0, 0.0).astype(BF)
    lane_j = lax.broadcasted_iota(jnp.int32, (1, 8 * SLOTS), 1)
    d_of = (lane_j * 205) >> 14
    rem = lane_j - d_of * SLOTS
    p_of = (rem * 205) >> 10
    s_of = (rem - p_of * CAP).astype(F32)
    e_of = (d_of >> 2) * 64 + (d_of & 3) * step + base
    spread = jnp.where(lax.broadcasted_iota(jnp.int32, (128, 8 * SLOTS), 0) == e_of, 1.0, 0.0).astype(BF)
    rank_at = jnp.dot(ranks, spread, preferred_element_type=F32)
    gate_at = jnp.dot(gates, spread, preferred_element_type=F32)
    prompt = lax.broadcasted_iota(jnp.int32, (512, 8 * SLOTS), 0) >> 5
    comb[...] = jnp.where((prompt == p_of) & (rank_at == s_of), gate_at, 0.0).astype(BF)

    for j in range(3):
        backs[j].wait_recv()
    mid = mid_ref[...]
    for j in range(3):
        mid = mid + p_in[j].astype(F32)
    mid_ref[...] = mid
    ms = jnp.mean(mid * mid, axis=1, keepdims=True)
    normed = (mid * lax.rsqrt(ms + 1e-6) * gain_ref[...]).astype(BF)

    def spots(c):
        def on_y(j):
            return up(y, j), at(r, l, a, up(y, j))

        def on_a(j):
            return up(a, j), at(r, l, up(a, j), y)

        return (a, y, on_a, on_y) if CHUNKS[c][2] else (y, a, on_y, on_a)

    first = [None] * len(CHUNKS)
    for c in TO_ORDER:
        m, n, _, inner = spots(c)
        gath[c][m, n] = normed[:, CHUNKS[c][0]:CHUNKS[c][0] + CHUNKS[c][1]]
        ref = gath[c].at[m, n]
        first[c] = [go(remote(ref, ref, s1s.at[c, j - 1], s1r.at[c, j - 1], inner(j)[1])) for j in range(1, 4)]

    second = [None] * len(CHUNKS)

    def spread_second(c):
        for cp in first[c]:
            cp.wait_recv()
        m, _, outer, _ = spots(c)
        ref = gath[c].at[m]
        second[c] = [go(remote(ref, ref, s2s.at[c, j - 1], s2r.at[c, j - 1], outer(j)[1])) for j in range(1, 4)]

    src = r * 4 + l
    third, local = [None] * len(CHUNKS), [None] * len(CHUNKS)

    def send_slots(c):
        fc = CHUNKS[c][1]
        for cp in second[c]:
            cp.wait_recv()
        if CHUNKS[c][2]:
            rows = jnp.concatenate([gath[c][i, k] for k in range(4) for i in range(4)], axis=0)
        else:
            rows = gath[c][...].reshape(512, fc)
        pack[c][...] = jnp.dot(sel[...], rows, preferred_element_type=F32).astype(BF).reshape(8, SLOTS, fc)
        cps = []
        for j in range(7):
            if j < 3:
                d, dev = r * 4 + up(l, j + 1), at(r, up(l, j + 1), a, y)
            else:
                d, dev = (1 - r) * 4 + up(l, j - 3), at(1 - r, up(l, j - 3), a, y)
            cps.append(go(remote(pack[c].at[d], block[c].at[src], ls.at[c, j], lr.at[c, j], dev)))
        third[c] = cps
        own = pltpu.make_async_copy(pack[c].at[src], block[c].at[src], locs.at[0, c])
        own.start()
        local[c] = own

    def gate_up(c, begin, end):
        fc = CHUNKS[c][1]
        for cp in third[c]:
            cp.wait_recv()
        local[c].wait()
        if begin:
            wcopies[0].wait()
            wcopies[1].wait()
        rows = block[c][...].reshape(8 * SLOTS, fc)
        at_f = slice(CHUNKS[c][0], CHUNKS[c][0] + CHUNKS[c][1])
        gp = jnp.dot(rows, wg[at_f, :], preferred_element_type=F32)
        upp = jnp.dot(rows, wu[at_f, :], preferred_element_type=F32)
        if begin:
            gacc[...] = gp
            uacc[...] = upp
        elif not end:
            gacc[...] += gp
            uacc[...] += upp
        else:
            gp = gp + gacc[...]
            act[...] = (gp * jax.nn.sigmoid(gp) * (upp + uacc[...])).astype(BF)

    for c in TO_ORDER:
        spread_second(c)
    last = len(CHUNKS) - 1
    for i, c in enumerate(SLOT_ORDER):
        send_slots(c)
        if i >= 1:
            gate_up(SLOT_ORDER[i - 1], i == 1, False)
    gate_up(SLOT_ORDER[last], False, True)

    wcopies[2].wait()
    back, b_local, h1, h2 = [None] * len(CHUNKS), [None] * len(CHUNKS), [None] * len(CHUNKS), [None] * len(CHUNKS)

    def down(c):
        f0, fc, _ = CHUNKS[c]
        o = jnp.dot(act[...], wd[:, f0:f0 + fc], preferred_element_type=F32).astype(BF)
        res[c][...] = o.reshape(8, SLOTS, fc)
        cps = []
        for j in range(7):
            if j < 3:
                s, d, dev = r * 4 + up(l, j + 1), r * 4 + l, at(r, up(l, j + 1), a, y)
            else:
                s, d, dev = (1 - r) * 4 + up(a, j - 3), r * 4 + a, at(1 - r, l, up(a, j - 3), y)
            cps.append(go(remote(res[c].at[s], ret[c].at[d], bs.at[c, j], br.at[c, j], dev)))
        back[c] = cps
        own = pltpu.make_async_copy(res[c].at[src], ret[c].at[src], locs.at[1, c])
        own.start()
        b_local[c] = own

    def combine(c):
        fc = CHUNKS[c][1]
        for cp in back[c]:
            cp.wait_recv()
        b_local[c].wait()
        o = jnp.dot(comb[...], ret[c][...].reshape(8 * SLOTS, fc), preferred_element_type=F32).astype(BF)
        if CHUNKS[c][2]:
            for p in range(16):
                part[c][p % 4, p // 4] = o[p * ROWS:(p + 1) * ROWS]
        else:
            part[c][...] = o.reshape(4, 4, ROWS, fc)
        _, _, outer, _ = spots(c)
        cps = []
        for j in range(1, 4):
            to, dev = outer(j)
            cps.append(go(remote(part[c].at[to], part_in[c].at[j - 1], h1s.at[c, j - 1], h1r.at[c, j - 1], dev)))
        h1[c] = cps

    def sum_one(c):
        for cp in h1[c]:
            cp.wait_recv()
        m, _, _, inner = spots(c)
        o = part[c][m].astype(F32)
        for j in range(3):
            o = o + part_in[c][j].astype(F32)
        half[c][...] = o.astype(BF)
        cps = []
        for j in range(1, 4):
            q, dev = inner(j)
            cps.append(go(remote(half[c].at[q], half_in[c].at[j - 1], h2s.at[c, j - 1], h2r.at[c, j - 1], dev)))
        h2[c] = cps

    def sum_two(c):
        for cp in h2[c]:
            cp.wait_recv()
        o = half[c][spots(c)[1]].astype(F32)
        for j in range(3):
            o = o + half_in[c][j].astype(F32)
        at_f = slice(CHUNKS[c][0], CHUNKS[c][0] + CHUNKS[c][1])
        out_ref[:, at_f] = (mid_ref[:, at_f] + o).astype(BF)

    stages = (down, combine, sum_one, sum_two)
    for t in range(len(CHUNKS) + 3):
        for n, stage in enumerate(stages):
            if 0 <= t - n < len(CHUNKS):
                stage(BACK_ORDER[t - n])
    for cp in pend:
        cp.wait_send()


def scratch():
    vm, dma, n = pltpu.VMEM, pltpu.SemaphoreType.DMA, len(CHUNKS)

    def each(*lead):
        return [vm((*lead, width), BF) for _, width, _ in CHUNKS]

    return [
        vm((ROWS, 4096), BF), vm((ROWS, 512), BF), vm((ROWS, 512), BF), vm((ROWS, D), BF),
        vm((GROUPS, T, HS), BF), vm((GROUPS, T, HS), BF), vm((HPG * HS, D), BF), vm((2, QR, T), F32),
        vm((GROUPS, ROWS, HPG * HS), BF), vm((3, ROWS, HPG * HS), BF), vm((3, ROWS, D), BF), vm((3, ROWS, D), BF),
        vm((ROWS, D), F32),
        vm((4, 4, ROWS, 256), BF), vm((D, FE), BF), vm((D, FE), BF), vm((FE, D), BF),
        vm((8 * SLOTS, FE), F32), vm((8 * SLOTS, FE), F32), vm((8 * SLOTS, FE), BF),
        vm((8 * SLOTS, 512), BF), vm((512, 8 * SLOTS), BF),
        each(4, 4, ROWS), each(8, SLOTS), each(8, SLOTS), each(8, SLOTS), each(8, SLOTS),
        each(4, 4, ROWS), each(3, 4, ROWS), each(4, ROWS), each(3, ROWS),
        dma((4,)), dma((GROUPS,)), dma((GROUPS,)), dma((4,)), dma((3,)), dma((3,)), dma((3,)), dma((3,)),
        dma((6,)), dma((6,)), dma((n, 3)), dma((n, 3)), dma((n, 3)), dma((n, 3)), dma((n, 7)), dma((n, 7)),
        dma((2, n)), dma((n, 7)), dma((n, 7)), dma((n, 3)), dma((n, 3)), dma((n, 3)), dma((n, 3)),
    ]


def layer_call(cid, *args):
    vmem, hbm = pl.BlockSpec(memory_space=pltpu.VMEM), pl.BlockSpec(memory_space=pl.ANY)
    return pl.pallas_call(
        layer_body,
        out_shape=jax.ShapeDtypeStruct((ROWS, D), BF),
        in_specs=[hbm] * 7 + [vmem] * 3 + [hbm] * 3,
        out_specs=vmem,
        scratch_shapes=scratch(),
        compiler_params=pltpu.CompilerParams(
            collective_id=cid, has_side_effects=True, vmem_limit_bytes=VMEM_LIMIT
        ),
        name="layer_%d" % cid,
    )(*args)


def per_device(queries, cache_keys, prompt_value_cache, new_keys, fresh_token_values, hidden, out_weight, norm_gain,
               expert_gate, expert_up, expert_down, expert_ids, routing_gates):
    out = layer_call(
        0, queries[0], cache_keys[0], prompt_value_cache[0], new_keys[0], fresh_token_values[0], hidden[0], out_weight,
        norm_gain[None, :], expert_ids[0].T, routing_gates[0].T, expert_gate[0], expert_up[0], expert_down[0],
    )
    return out[None]


def solution(mesh):
    split = P(("role", "row", "col"), None, None)
    return jax.shard_map(
        per_device,
        mesh=mesh,
        in_specs=(split,) * 6 + (P("row", None), P()) + (split,) * 5,
        out_specs=split,
        check_vma=False,
    )
```

```python
import jax
import jax.numpy as jnp
from jax import lax
from jax.experimental import pallas as pl
from jax.experimental.pallas import tpu as pltpu
from jax.sharding import PartitionSpec as P

MESH = pl.DeviceIdType.MESH
BF, F32 = jnp.bfloat16, jnp.float32

D = 2048
HS = 128
GROUPS = 4
HPG = 8
ROWS = 32
T = 4096
FE = 768
CAP = 5
SLOTS = 16 * CAP
QR = ROWS * HPG
TC = 1024
CHUNKS = ((0, 768, True), (768, 768, False), (1536, 512, False))
TO_ORDER = (1, 0, 2)
SLOT_ORDER = (0, 1, 2)
BACK_ORDER = (2, 1, 0)
VMEM_LIMIT = 60 * 2**20
LOG2E = 1.4426950408889634


def where_am_i():
    r, x, col = lax.axis_index("role"), lax.axis_index("row"), lax.axis_index("col")
    return r, x, lax.div(col, 4), lax.rem(col, 4)


def up(v, j):
    return jnp.where(v + j > 3, v + j - 4, v + j)


def remote(src, dst, send, recv, dev):
    return pltpu.make_async_remote_copy(
        src_ref=src, dst_ref=dst, send_sem=send, recv_sem=recv, device_id=dev, device_id_type=MESH
    )


def layer_body(q_hbm, k_hbm, v_hbm, nk_hbm, nv_hbm, hid_hbm, w_hbm, gain_ref, ids_ref, gates_ref, wg_hbm, wu_hbm,
               wd_hbm, out_ref,
               qv, nkv, nvv, hidv, kv, vv, wv, sc, a_out, a_in, p_out, p_in, mid_ref,
               tab, wg, wu, wd, gacc, uacc, act, sel, comb, gath, pack, block, res, ret, part, part_in, half, half_in,
               insem, ksem, vsem, wsem, as_sem, ar_sem, ps_sem, pr_sem,
               ts, tr, s1s, s1r, s2s, s2r, ls, lr, locs, bs, br, h1s, h1r, h2s, h2r):
    r, x, z, y = where_am_i()
    col = z * 4 + y
    a = jnp.where(r == 0, z, x)
    l = jnp.where(r == 0, x, z)

    def at(role, l_, a_, y_):
        xx = jnp.where(r == 0, l_, a_)
        zz = jnp.where(r == 0, a_, l_)
        return (role, xx, zz * 4 + y_)

    def load(src, dst, sem):
        return pltpu.make_async_copy(src, dst, sem)

    kloads, vloads = [], []
    for j in range(GROUPS):
        cols = pl.ds(pl.multiple_of(up(x, 1 + j) * HS, HS), HS)
        kloads.append(load(k_hbm.at[:, cols], kv.at[j], ksem.at[j]))
        vloads.append(load(v_hbm.at[:, cols], vv.at[j], vsem.at[j]))
    ins = [load(q_hbm, qv, insem.at[0]), load(nk_hbm, nkv, insem.at[1]), load(nv_hbm, nvv, insem.at[2]),
           load(hid_hbm, hidv, insem.at[3])]
    cw = load(w_hbm, wv, wsem.at[3])
    wcopies = [load(wg_hbm, wg, wsem.at[0]), load(wu_hbm, wu, wsem.at[1]), load(wd_hbm, wd, wsem.at[2])]
    for cp in ins:
        cp.start()
    kloads[0].start()
    vloads[0].start()
    kloads[1].start()

    barrier = pltpu.get_barrier_semaphore()
    partners = [at(1 - r, l, a, y)]
    for j in range(1, 4):
        partners += [at(r, up(l, j), a, y), at(r, l, up(a, j), y), at(r, l, a, up(y, j)),
                     at(1 - r, up(l, j), a, y), at(1 - r, l, up(a, j), y)]
    for dev in partners:
        pl.semaphore_signal(barrier, inc=1, device_id=dev, device_id_type=MESH)

    expert = lax.broadcasted_iota(jnp.int32, (128, ROWS), 0)
    named_t = jnp.zeros((128, ROWS), F32)
    gate_t = jnp.zeros((128, ROWS), F32)
    for k in range(8):
        hit = ids_ref[k:k + 1, :] == expert
        named_t = jnp.where(hit, 1.0, named_t)
        gate_t = jnp.where(hit, gates_ref[k:k + 1, :], gate_t)
    sq0 = lax.broadcasted_iota(jnp.int32, (ROWS, ROWS), 0)
    sq1 = lax.broadcasted_iota(jnp.int32, (ROWS, ROWS), 1)
    before = jnp.where(sq0 > sq1, 1.0, 0.0).astype(BF)
    same_row = jnp.where(sq0 == sq1, 1.0, 0.0).astype(BF)

    def rows_of(left, right):
        return lax.dot_general(left, right.astype(BF), (((1,), (1,)), ((), ())), preferred_element_type=F32)

    tab[y, a, :, 0:128] = jnp.where(rows_of(same_row, named_t) > 0, rows_of(before, named_t), -1.0).astype(BF)
    tab[y, a, :, 128:256] = rows_of(same_row, gate_t).astype(BF)

    pend = []

    def go(cp):
        cp.start()
        pend.append(cp)
        return cp

    t1, t2 = [], []

    scale = HS ** -0.5 * LOG2E
    outs, backs = [], []

    def serve(j):
        outs[j].wait_recv()
        if j == 0:
            cw.wait()
        p_out[j] = jnp.dot(a_in[j], wv[...], preferred_element_type=F32).astype(BF)
        backs.append(go(remote(p_out.at[j], p_in.at[j], ps_sem.at[j], pr_sem.at[j], (r, up(x, 3 - j), col))))

    def block_of(j):
        g = up(x, 1 + j)
        q = jnp.concatenate(
            [qv[:, pl.ds(pl.multiple_of(g * (HPG * HS) + h * HS, HS), HS)] for h in range(HPG)], axis=0
        )
        own_k = jnp.concatenate([nkv[:, pl.ds(pl.multiple_of(g * HS, HS), HS)]] * HPG, axis=0)
        return q, jnp.sum(q.astype(F32) * own_k.astype(F32), axis=1, keepdims=True)

    def keys_at(i):
        return pl.ds(pl.multiple_of(i * TC, TC), TC)

    def score(j, i, q, m):
        s = lax.dot_general(q, kv[j, keys_at(i), :], (((1,), (1,)), ((), ())), preferred_element_type=F32)
        sc[j % 2, :, keys_at(i)] = s
        for b in range(TC // HS):
            m = jnp.maximum(m, s[:, b * HS:(b + 1) * HS])
        return m

    def mix(j, i, top, acc, den):
        e = jnp.exp2((sc[j % 2, :, keys_at(i)] - top) * scale)
        for b in range(TC // HS):
            den = den + e[:, b * HS:(b + 1) * HS]
        return acc + jnp.dot(e.astype(BF), vv[j, keys_at(i), :], preferred_element_type=F32), den

    low, zero = jnp.full((QR, HS), -jnp.inf, F32), jnp.zeros((QR, HS), F32)
    for cp in ins[:3]:
        cp.wait()
    kloads[0].wait()
    q, own = block_of(0)
    m = lax.fori_loop(0, T // TC, lambda i, m: score(0, i, q, m), low)
    for j in range(GROUPS):
        g = up(x, 1 + j)
        own_v = jnp.concatenate([nvv[:, pl.ds(pl.multiple_of(g * HS, HS), HS)]] * HPG, axis=0)
        top = jnp.maximum(jnp.max(m, axis=1, keepdims=True), own)
        vloads[j].wait()
        if j + 2 < GROUPS:
            kloads[j + 2].start()
        if j + 1 < GROUPS:
            vloads[j + 1].start()
        if j == 0:
            cw.start()
        if j == 2:
            for cp in wcopies:
                cp.start()
        if j + 1 < GROUPS:
            kloads[j + 1].wait()
            q, next_own = block_of(j + 1)

            def both(i, carry):
                m, acc, den = carry
                m = score(j + 1, i, q, m)
                return m, *mix(j, i, top, acc, den)

            m, acc, den = lax.fori_loop(0, T // TC, both, (low, zero, zero))
        else:
            next_own = None
            acc, den = lax.fori_loop(0, T // TC, lambda i, carry: mix(j, i, top, *carry), (zero, zero))
        own_e = jnp.exp2((own - top) * scale)
        total = jnp.sum(den, axis=1, keepdims=True) + own_e
        att = ((acc + own_e * own_v.astype(F32)) / total).astype(BF)
        for h in range(HPG):
            a_out[j, :, h * HS:(h + 1) * HS] = att[h * ROWS:(h + 1) * ROWS]
        if j == 0:
            pl.semaphore_wait(barrier, len(partners))
        if j < 3:
            outs.append(go(remote(a_out.at[j], a_in.at[j], as_sem.at[j], ar_sem.at[j], (r, g, col))))
        if j == 0:
            for i in range(1, 4):
                t1.append(go(remote(tab.at[y, a], tab.at[y, a], ts.at[i - 1], tr.at[i - 1], at(r, l, up(a, i), y))))
        if j == 1:
            for cp in t1:
                cp.wait_recv()
            for i in range(1, 4):
                t2.append(go(remote(tab.at[y], tab.at[y], ts.at[i + 2], tr.at[i + 2], at(r, l, a, up(y, i)))))
        if j >= 1:
            serve(j - 1)
        own = next_own

    ins[3].wait()
    mid = hidv[...].astype(F32) + jnp.dot(a_out[3], wv[...], preferred_element_type=F32)
    mid_ref[...] = mid

    for cp in t2:
        cp.wait_recv()
    step = jnp.where(r == 0, 16, 4)
    base = jnp.where(r == 0, z * 4 + y, x * 16 + y)
    ranks = tab[:, :, :, 0:128].reshape(512, 128)
    gates = tab[:, :, :, 128:256].reshape(512, 128)
    d8 = lax.broadcasted_iota(jnp.int32, (8, 128), 0)
    e8 = lax.broadcasted_iota(jnp.int32, (8, 128), 1)
    pick = jnp.where(e8 == (d8 >> 2) * 64 + (d8 & 3) * step + base, 1.0, 0.0).astype(BF)
    by_lane = lax.dot_general(pick, ranks, (((1,), (1,)), ((), ())), preferred_element_type=F32)
    slot = lax.broadcasted_iota(jnp.int32, (SLOTS, 512), 0)
    its_prompt = (slot * 205) >> 10
    same = its_prompt == (lax.broadcasted_iota(jnp.int32, (SLOTS, 512), 1) >> 5)
    want = jnp.where(same, slot - its_prompt * CAP, -7).astype(F32)
    for d in range(8):
        sel[d * SLOTS:(d + 1) * SLOTS, :] = jnp.where(want == by_lane[d:d + 1, :], 1.0, 0.0).astype(BF)
    lane_j = lax.broadcasted_iota(jnp.int32, (1, 8 * SLOTS), 1)
    d_of = (lane_j * 205) >> 14
    rem = lane_j - d_of * SLOTS
    p_of = (rem * 205) >> 10
    s_of = (rem - p_of * CAP).astype(F32)
    e_of = (d_of >> 2) * 64 + (d_of & 3) * step + base
    spread = jnp.where(lax.broadcasted_iota(jnp.int32, (128, 8 * SLOTS), 0) == e_of, 1.0, 0.0).astype(BF)
    rank_at = jnp.dot(ranks, spread, preferred_element_type=F32)
    gate_at = jnp.dot(gates, spread, preferred_element_type=F32)
    prompt = lax.broadcasted_iota(jnp.int32, (512, 8 * SLOTS), 0) >> 5
    comb[...] = jnp.where((prompt == p_of) & (rank_at == s_of), gate_at, 0.0).astype(BF)

    for j in range(3):
        backs[j].wait_recv()
    mid = mid_ref[...]
    for j in range(3):
        mid = mid + p_in[j].astype(F32)
    mid_ref[...] = mid
    ms = jnp.mean(mid * mid, axis=1, keepdims=True)
    normed = (mid * lax.rsqrt(ms + 1e-6) * gain_ref[...]).astype(BF)

    def spots(c):
        def on_y(j):
            return up(y, j), at(r, l, a, up(y, j))

        def on_a(j):
            return up(a, j), at(r, l, up(a, j), y)

        return (a, y, on_a, on_y) if CHUNKS[c][2] else (y, a, on_y, on_a)

    first = [None] * len(CHUNKS)
    for c in TO_ORDER:
        m, n, _, inner = spots(c)
        gath[c][m, n] = normed[:, CHUNKS[c][0]:CHUNKS[c][0] + CHUNKS[c][1]]
        ref = gath[c].at[m, n]
        first[c] = [go(remote(ref, ref, s1s.at[c, j - 1], s1r.at[c, j - 1], inner(j)[1])) for j in range(1, 4)]

    second = [None] * len(CHUNKS)

    def spread_second(c):
        for cp in first[c]:
            cp.wait_recv()
        m, _, outer, _ = spots(c)
        ref = gath[c].at[m]
        second[c] = [go(remote(ref, ref, s2s.at[c, j - 1], s2r.at[c, j - 1], outer(j)[1])) for j in range(1, 4)]

    src = r * 4 + l
    third, local = [None] * len(CHUNKS), [None] * len(CHUNKS)

    def send_slots(c):
        fc = CHUNKS[c][1]
        for cp in second[c]:
            cp.wait_recv()
        if CHUNKS[c][2]:
            rows = jnp.concatenate([gath[c][i, k] for k in range(4) for i in range(4)], axis=0)
        else:
            rows = gath[c][...].reshape(512, fc)
        pack[c][...] = jnp.dot(sel[...], rows, preferred_element_type=F32).astype(BF).reshape(8, SLOTS, fc)
        cps = []
        for j in range(7):
            if j < 3:
                d, dev = r * 4 + up(l, j + 1), at(r, up(l, j + 1), a, y)
            else:
                d, dev = (1 - r) * 4 + up(l, j - 3), at(1 - r, up(l, j - 3), a, y)
            cps.append(go(remote(pack[c].at[d], block[c].at[src], ls.at[c, j], lr.at[c, j], dev)))
        third[c] = cps
        own = pltpu.make_async_copy(pack[c].at[src], block[c].at[src], locs.at[0, c])
        own.start()
        local[c] = own

    def gate_up(c, begin, end):
        fc = CHUNKS[c][1]
        for cp in third[c]:
            cp.wait_recv()
        local[c].wait()
        if begin:
            wcopies[0].wait()
            wcopies[1].wait()
        rows = block[c][...].reshape(8 * SLOTS, fc)
        at_f = slice(CHUNKS[c][0], CHUNKS[c][0] + CHUNKS[c][1])
        gp = jnp.dot(rows, wg[at_f, :], preferred_element_type=F32)
        upp = jnp.dot(rows, wu[at_f, :], preferred_element_type=F32)
        if begin:
            gacc[...] = gp
            uacc[...] = upp
        elif not end:
            gacc[...] += gp
            uacc[...] += upp
        else:
            gp = gp + gacc[...]
            act[...] = (gp * jax.nn.sigmoid(gp) * (upp + uacc[...])).astype(BF)

    for c in TO_ORDER:
        spread_second(c)
    last = len(CHUNKS) - 1
    for i, c in enumerate(SLOT_ORDER):
        send_slots(c)
        if i >= 1:
            gate_up(SLOT_ORDER[i - 1], i == 1, False)
    gate_up(SLOT_ORDER[last], False, True)

    wcopies[2].wait()
    back, b_local, h1, h2 = [None] * len(CHUNKS), [None] * len(CHUNKS), [None] * len(CHUNKS), [None] * len(CHUNKS)

    def down(c):
        f0, fc, _ = CHUNKS[c]
        o = jnp.dot(act[...], wd[:, f0:f0 + fc], preferred_element_type=F32).astype(BF)
        res[c][...] = o.reshape(8, SLOTS, fc)
        cps = []
        for j in range(7):
            if j < 3:
                s, d, dev = r * 4 + up(l, j + 1), r * 4 + l, at(r, up(l, j + 1), a, y)
            else:
                s, d, dev = (1 - r) * 4 + up(a, j - 3), r * 4 + a, at(1 - r, l, up(a, j - 3), y)
            cps.append(go(remote(res[c].at[s], ret[c].at[d], bs.at[c, j], br.at[c, j], dev)))
        back[c] = cps
        own = pltpu.make_async_copy(res[c].at[src], ret[c].at[src], locs.at[1, c])
        own.start()
        b_local[c] = own

    def combine(c):
        fc = CHUNKS[c][1]
        for cp in back[c]:
            cp.wait_recv()
        b_local[c].wait()
        o = jnp.dot(comb[...], ret[c][...].reshape(8 * SLOTS, fc), preferred_element_type=F32).astype(BF)
        if CHUNKS[c][2]:
            for p in range(16):
                part[c][p % 4, p // 4] = o[p * ROWS:(p + 1) * ROWS]
        else:
            part[c][...] = o.reshape(4, 4, ROWS, fc)
        _, _, outer, _ = spots(c)
        cps = []
        for j in range(1, 4):
            to, dev = outer(j)
            cps.append(go(remote(part[c].at[to], part_in[c].at[j - 1], h1s.at[c, j - 1], h1r.at[c, j - 1], dev)))
        h1[c] = cps

    def sum_one(c):
        for cp in h1[c]:
            cp.wait_recv()
        m, _, _, inner = spots(c)
        o = part[c][m].astype(F32)
        for j in range(3):
            o = o + part_in[c][j].astype(F32)
        half[c][...] = o.astype(BF)
        cps = []
        for j in range(1, 4):
            q, dev = inner(j)
            cps.append(go(remote(half[c].at[q], half_in[c].at[j - 1], h2s.at[c, j - 1], h2r.at[c, j - 1], dev)))
        h2[c] = cps

    def sum_two(c):
        for cp in h2[c]:
            cp.wait_recv()
        o = half[c][spots(c)[1]].astype(F32)
        for j in range(3):
            o = o + half_in[c][j].astype(F32)
        at_f = slice(CHUNKS[c][0], CHUNKS[c][0] + CHUNKS[c][1])
        out_ref[:, at_f] = (mid_ref[:, at_f] + o).astype(BF)

    stages = (down, combine, sum_one, sum_two)
    sent = list(pend)
    for t in range(len(CHUNKS) + 3):
        for n, stage in enumerate(stages):
            if 0 <= t - n < len(CHUNKS):
                stage(BACK_ORDER[t - n])
                if t == 0 or (n == 2 and t - n == len(CHUNKS) - 1):
                    sent = sent if t == 0 else pend[:-3]
                    del pend[:len(sent)]
                    for cp in sent:
                        cp.wait_send()
                    sent = []
    for cp in pend:
        cp.wait_send()


def scratch():
    vm, dma, n = pltpu.VMEM, pltpu.SemaphoreType.DMA, len(CHUNKS)

    def each(*lead):
        return [vm((*lead, width), BF) for _, width, _ in CHUNKS]

    return [
        vm((ROWS, 4096), BF), vm((ROWS, 512), BF), vm((ROWS, 512), BF), vm((ROWS, D), BF),
        vm((GROUPS, T, HS), BF), vm((GROUPS, T, HS), BF), vm((HPG * HS, D), BF), vm((2, QR, T), F32),
        vm((GROUPS, ROWS, HPG * HS), BF), vm((3, ROWS, HPG * HS), BF), vm((3, ROWS, D), BF), vm((3, ROWS, D), BF),
        vm((ROWS, D), F32),
        vm((4, 4, ROWS, 256), BF), vm((D, FE), BF), vm((D, FE), BF), vm((FE, D), BF),
        vm((8 * SLOTS, FE), F32), vm((8 * SLOTS, FE), F32), vm((8 * SLOTS, FE), BF),
        vm((8 * SLOTS, 512), BF), vm((512, 8 * SLOTS), BF),
        each(4, 4, ROWS), each(8, SLOTS), each(8, SLOTS), each(8, SLOTS), each(8, SLOTS),
        each(4, 4, ROWS), each(3, 4, ROWS), each(4, ROWS), each(3, ROWS),
        dma((4,)), dma((GROUPS,)), dma((GROUPS,)), dma((4,)), dma((3,)), dma((3,)), dma((3,)), dma((3,)),
        dma((6,)), dma((6,)), dma((n, 3)), dma((n, 3)), dma((n, 3)), dma((n, 3)), dma((n, 7)), dma((n, 7)),
        dma((2, n)), dma((n, 7)), dma((n, 7)), dma((n, 3)), dma((n, 3)), dma((n, 3)), dma((n, 3)),
    ]


def layer_call(cid, *args):
    vmem, hbm = pl.BlockSpec(memory_space=pltpu.VMEM), pl.BlockSpec(memory_space=pl.ANY)
    return pl.pallas_call(
        layer_body,
        out_shape=jax.ShapeDtypeStruct((ROWS, D), BF),
        in_specs=[hbm] * 7 + [vmem] * 3 + [hbm] * 3,
        out_specs=vmem,
        scratch_shapes=scratch(),
        compiler_params=pltpu.CompilerParams(
            collective_id=cid, has_side_effects=True, vmem_limit_bytes=VMEM_LIMIT
        ),
        name="layer_%d" % cid,
    )(*args)


def per_device(queries, cache_keys, prompt_value_cache, new_keys, fresh_token_values, hidden, out_weight, norm_gain,
               expert_gate, expert_up, expert_down, expert_ids, routing_gates):
    out = layer_call(
        0, queries[0], cache_keys[0], prompt_value_cache[0], new_keys[0], fresh_token_values[0], hidden[0], out_weight,
        norm_gain[None, :], expert_ids[0].T, routing_gates[0].T, expert_gate[0], expert_up[0], expert_down[0],
    )
    return out[None]


def solution(mesh):
    split = P(("role", "row", "col"), None, None)
    return jax.shard_map(
        per_device,
        mesh=mesh,
        in_specs=(split,) * 6 + (P("row", None), P()) + (split,) * 5,
        out_specs=split,
        check_vma=False,
    )
```
